32 devices in a mesh: row: 8 (over z, core), col: 4 (over y, x).
Axes of the slice: x: 2, y: 2, z: 4, core: 2. Of those that a mesh axis runs over, the one named last changes fastest.
Arguments:
- tokens: bfloat16 [2048, 14336], P('row'), may hold values from -6 to 6
- qkv_weight: bfloat16 [14336, 4, 8, 336], P(None, 'col', 'row'), may hold values from -0.046875 to 0.046875
- qkv_bias: float32 [10752], P('col'), may hold values from -6 to 6
Outputs:
- joined_qkv: bfloat16 [2048, 10752], P('row', 'col')
The draws below stay inside these ranges and needn't reach their ends.
All inputs are finite; a program needn't handle non-finite values.
Results may differ from the reference program's by a relative error of at most 0.01.
Values may be sent and summed in bfloat16 or wider, within the bound.
No kernel may reach another device: no remote copies, remote signals or barrier semaphores. Data moves between devices by JAX's collectives and lax.ppermute only.
A program may use at most 128 MiB of HBM per device.

```python
import jax
import jax.numpy as jnp

D = 14336
OUT = 10752
SUBW = 336
TOKENS = 2048
N_ROW = 8
N_COL = 4


def block_scale(key, extent, split, smallest, high):
    level, own = 1.0, jax.random.fold_in(key, 6)
    for dim, shards_of in split:
        heights = jnp.exp(jax.random.uniform(jax.random.fold_in(own, dim), (shards_of,), jnp.float32, smallest / len(split), high / len(split)))
        level = level * jnp.repeat(heights, extent[dim] // shards_of).reshape([-1 if axis == dim else 1 for axis in range(len(extent))])
    return level


def noise(stream_key, extent, spread, most, pieces=(), kind=jnp.bfloat16):
    drawn = spread * jax.random.normal(stream_key, extent, jnp.float32)
    if pieces:
        drawn = drawn * block_scale(stream_key, extent, pieces, -0.22, 0.18)
    return jnp.clip(drawn, -most, most).astype(kind)


def setup_inputs(seed: int = 0) -> dict:
    key_list = jax.random.split(jax.random.key(seed), 4)
    return {
        "tokens": noise(key_list[0], (TOKENS, D), 1.0, 6.0, ((0, 8),)),
        "qkv_weight": noise(key_list[1], (D, N_COL, N_ROW, SUBW), D ** -0.5, 0.046875, ((1, 4), (2, 8))),
        "qkv_bias": noise(key_list[2], (OUT,), 1.0, 6.0, ((0, 4),), jnp.float32),
    }


def reference(tokens, qkv_weight, qkv_bias):
    weights = qkv_weight.reshape(D, OUT)
    band_rows = D // N_ROW
    running = jnp.zeros((TOKENS, OUT), jnp.float32)
    for shard in range(N_ROW):
        partial_value = jnp.dot(tokens[:, shard * band_rows:(shard + 1) * band_rows],
                          weights[shard * band_rows:(shard + 1) * band_rows, :],
                          preferred_element_type=jnp.float32).astype(jnp.bfloat16)
        running = running + partial_value.astype(jnp.float32)
    return (running + qkv_bias[None, :]).astype(jnp.bfloat16)
```

```python
import functools

import jax
import jax.numpy as jnp
from jax import lax
from jax.experimental import pallas as pl
from jax.experimental.pallas import tpu as pltpu
from jax.sharding import PartitionSpec as P

VMEM = 56 * 1024 * 1024


def divisor(size, most):
    return max(d for d in range(128, most + 1, 128) if size % d == 0)


def product_kernel(n_w, n_t, *refs):
    w_refs, t_refs = refs[:n_w], refs[n_w : n_w + n_t]
    out_ref, total = refs[-2], refs[-1]
    step = pl.program_id(0)

    @pl.when(step == 0)
    def _():
        total[...] = jnp.zeros_like(total)

    rows = t_refs[0].shape[0]
    for i, w in enumerate(w_refs):
        for k, t in enumerate(t_refs):
            total[i, :, k * rows : (k + 1) * rows] += lax.dot_general(
                w[...], t[...], (((1,), (1,)), ((), ())), preferred_element_type=jnp.float32
            )

    @pl.when(step == pl.num_programs(0) - 1)
    def _():
        out_ref[...] = total[...].astype(out_ref.dtype)


def products(ws, ts, dtype):
    m, depth = ws[0].shape
    rows = ts[0].shape[0]
    block = divisor(depth, 1024)
    shape = (len(ws), m, rows * len(ts))
    return pl.pallas_call(
        functools.partial(product_kernel, len(ws), len(ts)),
        grid=(depth // block,),
        in_specs=[pl.BlockSpec((m, block), lambda i: (0, i)) for _ in ws]
        + [pl.BlockSpec((rows, block), lambda i: (0, i)) for _ in ts],
        out_specs=pl.BlockSpec(shape, lambda i: (0, 0, 0)),
        out_shape=jax.ShapeDtypeStruct(shape, dtype),
        scratch_shapes=[pltpu.VMEM(shape, jnp.float32)],
        compiler_params=pltpu.CompilerParams(vmem_limit_bytes=VMEM),
        cost_estimate=pl.CostEstimate(
            flops=2 * len(ws) * m * rows * len(ts) * depth,
            bytes_accessed=2 * depth * (m * len(ws) + rows * len(ts)) + 2 * len(ws) * m * rows * len(ts),
            transcendentals=0,
        ),
    )(*ws, *ts)


def join_kernel(n, *refs):
    part_refs, bias_ref, out_ref, joined = refs[:n], refs[n], refs[n + 1], refs[n + 2]
    m = part_refs[0].shape[0]
    me = lax.axis_index("row")
    for j, part in enumerate(part_refs):
        joined[pl.ds(pl.multiple_of((me ^ j) * m, 8), m), :] = part[...].astype(jnp.float32)
    block = divisor(out_ref.shape[1], 512)
    for i in range(out_ref.shape[1] // block):
        cols = slice(i * block, (i + 1) * block)
        out_ref[:, cols] = (joined[cols, :].T + bias_ref[:, cols]).astype(out_ref.dtype)


def join(parts, bias):
    m, rows = parts[0].shape
    n = len(parts)
    return pl.pallas_call(
        functools.partial(join_kernel, n),
        out_shape=jax.ShapeDtypeStruct((rows, n * m), jnp.bfloat16),
        in_specs=[pl.BlockSpec(memory_space=pltpu.VMEM)] * (n + 1),
        out_specs=pl.BlockSpec(memory_space=pltpu.VMEM),
        scratch_shapes=[pltpu.VMEM((n * m, rows), jnp.float32)],
        compiler_params=pltpu.CompilerParams(vmem_limit_bytes=VMEM),
        cost_estimate=pl.CostEstimate(flops=n * m * rows, bytes_accessed=4 * n * m * rows, transcendentals=0),
    )(*parts, bias[None, :])


def shards(tokens, qkv_weight, qkv_bias):
    n_row, n_col = lax.axis_size("row"), lax.axis_size("col")
    row, col = lax.axis_index("row"), lax.axis_index("col")
    planes = n_row // 2
    plane = row // 2
    feats = tokens.shape[1]
    band = feats // n_col
    weight = qkv_weight.reshape(feats, -1).T
    columns = weight.shape[0]

    def flip_col(x, j):
        return lax.ppermute(x, "col", [(i, i ^ j) for i in range(n_col)])

    def flip_row(x, j):
        return lax.ppermute(x, "row", [(i, i ^ j) for i in range(n_row)])

    own = lax.dynamic_slice_in_dim(tokens, col * band, band, 1)
    held = []
    last = {0: own, 1: own}
    for s in range(1, planes):
        now = {}
        for parity in (0, 1):
            pairs, came = [], {}
            for p in range(parity, planes - 1, 2):
                if p - s + 1 >= 0:
                    pairs.append((p, p + 1))
                    came[p + 1] = p - s + 1
                if p + s < planes:
                    pairs.append((p + 1, p))
                    came[p] = p + s
            if pairs:
                sent = last[1 - parity]
                now[parity] = lax.ppermute(sent, "row", [(2 * a + c, 2 * b + c) for a, b in pairs for c in (0, 1)])
                held.append((now[parity], came))
        last = now

    w_band = [lax.dynamic_slice_in_dim(weight, (col ^ j) * band, band, 1) for j in range(n_col)]
    w_band = [w_band[0]] + [flip_col(w_band[j], j) for j in range(1, n_col)]

    def arrived(d):
        wanted = [next(i for i, (_, came) in enumerate(held) if came.get(p) == p ^ d) for p in range(planes)]
        value = held[wanted[0]][0]
        for i in sorted(set(wanted) - {wanted[0]}):
            mine = functools.reduce(jnp.logical_or, [plane == p for p in range(planes) if wanted[p] == i])
            value = jnp.where(mine, held[i][0], value)
        return value

    half = tokens.shape[0]
    parts = [None] * n_row
    here = products([weight], [tokens, flip_row(tokens, 1)], jnp.bfloat16)[0]
    parts[0] = here[:, :half]
    parts[1] = flip_row(here[:, half:], 1)

    bits = [1 << b for b in range(n_col.bit_length() - 1)]
    for d in range(1, planes):
        same = arrived(d)
        both = [same, flip_row(same, 1)]
        order = bits[d % len(bits) :] + bits[: d % len(bits)]
        out = [j for j in range(n_col) if j & order[0]]
        kept = [j for j in range(n_col) if not j & order[0]]
        sent = products([w_band[j] for j in out], both, jnp.bfloat16)
        mine = products([w_band[j] for j in kept], both, jnp.float32)
        for n, bit in enumerate(order):
            got = flip_col(sent, bit).astype(jnp.float32)
            mine = mine + got
            if n + 1 < len(order):
                nxt = order[n + 1]
                go = [i for i, j in enumerate(kept) if j & nxt]
                stay = [i for i, j in enumerate(kept) if not j & nxt]
                sent = jnp.stack([mine[i] for i in go]).astype(jnp.bfloat16)
                mine = jnp.stack([mine[i] for i in stay])
                kept = [kept[i] for i in stay]
        done = mine[0].astype(jnp.bfloat16)
        parts[2 * d] = flip_row(done[:, :half], 2 * d)
        parts[2 * d + 1] = flip_row(done[:, half:], 2 * d + 1)
    return join(parts, qkv_bias)


def solution(mesh):
    return jax.shard_map(
        shards,
        mesh=mesh,
        in_specs=(P("row", None), P(None, "col", "row", None), P("col")),
        out_specs=P("row", "col"),
        check_vma=False,
    )
```

```python
import functools

import jax
import jax.numpy as jnp
from jax import lax
from jax.experimental import pallas as pl
from jax.experimental.pallas import tpu as pltpu
from jax.sharding import PartitionSpec as P

ROOM = 14 * 1024 * 1024
SPACE = 0
GATE = 0
GATE2 = 0
IN_VMEM = pl.BlockSpec(memory_space=pltpu.VMEM)
IN_HBM = pl.BlockSpec(memory_space=pltpu.HBM)
ANYWHERE = pl.BlockSpec(memory_space=pl.ANY)
BOTH_LAST = (((1,), (1,)), ((), ()))


def divisor(size, most):
    return max(d for d in range(128, most + 1, 128) if size % d == 0)


def bands_kernel(pieces, band, x, *refs):
    outs, sems = refs[-1 - len(pieces) : -1], refs[-1]
    col = lax.axis_index("col")
    copies = []
    for i, (j, first, rows) in enumerate(pieces):
        start = pl.multiple_of((col ^ j) * band, 128)
        copies.append(pltpu.make_async_copy(x.at[pl.ds(first, rows), pl.ds(start, band)], outs[i], sems.at[i]))
    for copy in copies:
        copy.start()
    for copy in copies:
        copy.wait()


def bands(x, pieces, n_col, after):
    band = x.shape[1] // n_col
    return pl.pallas_call(
        functools.partial(bands_kernel, pieces, band),
        out_shape=[jax.ShapeDtypeStruct((rows, band), x.dtype) for _, _, rows in pieces],
        in_specs=[IN_HBM] + [ANYWHERE] * len(after),
        out_specs=[IN_VMEM] * len(pieces),
        scratch_shapes=[pltpu.SemaphoreType.DMA((len(pieces),))],
        compiler_params=pltpu.CompilerParams(vmem_limit_bytes=ROOM),
    )(pltpu.with_memory_space_constraint(x, pltpu.HBM), *after)


def choose_kernel(wanted, n, *refs):
    x_refs, outs, sem = refs[:n], refs[n:-1], refs[-1]
    plane = lax.axis_index("row") // 2
    for i, x in enumerate(x_refs):
        here = functools.reduce(jnp.logical_or, [plane == p for p, w in enumerate(wanted) if w == i])

        @pl.when(here)
        def _():
            first, copies = 0, []
            for k, out in enumerate(outs):
                width = out.shape[1]
                copies.append(pltpu.make_async_copy(x.at[:, pl.ds(first, width)], out, sem.at[k]))
                first += width
            for copy in copies:
                copy.start()
            for copy in copies:
                copy.wait()


def choose(xs, wanted, after, cuts):
    rows, width = xs[0].shape
    return pl.pallas_call(
        lambda *refs: choose_kernel(wanted, len(xs), *refs[: len(xs)], *refs[len(xs) + len(after) :]),
        out_shape=[jax.ShapeDtypeStruct((rows, width // cuts), xs[0].dtype)] * cuts,
        in_specs=[ANYWHERE] * (len(xs) + len(after)),
        out_specs=[IN_VMEM] * cuts,
        scratch_shapes=[pltpu.SemaphoreType.DMA((cuts,))],
        compiler_params=pltpu.CompilerParams(vmem_limit_bytes=ROOM),
    )(*xs, *after)


def pass_kernel(*refs):
    pass


def passed(xs, after, flops):
    return pl.pallas_call(
        pass_kernel,
        out_shape=[jax.ShapeDtypeStruct(x.shape, x.dtype) for x in xs],
        in_specs=[ANYWHERE] * (len(xs) + len(after)),
        out_specs=[ANYWHERE] * len(xs),
        input_output_aliases={i: i for i in range(len(xs))},
        compiler_params=pltpu.CompilerParams(vmem_limit_bytes=ROOM),
        cost_estimate=pl.CostEstimate(flops=flops, bytes_accessed=0, transcendentals=0),
    )(*xs, *after)


def gate_kernel(*refs):
    refs[-1][...] = jnp.zeros_like(refs[-1])


def gate(after, flops):
    return pl.pallas_call(
        gate_kernel,
        out_shape=jax.ShapeDtypeStruct((8, 128), jnp.float32),
        in_specs=[ANYWHERE] * len(after),
        out_specs=IN_VMEM,
        compiler_params=pltpu.CompilerParams(vmem_limit_bytes=ROOM),
        cost_estimate=pl.CostEstimate(flops=flops, bytes_accessed=0, transcendentals=0),
    )(*after)


def deep_kernel(w, t0, t1, out_ref, total):
    step = pl.program_id(0)

    @pl.when(step == 0)
    def _():
        total[...] = jnp.zeros_like(total)

    rows = t0.shape[0]
    for k, t in enumerate((t0, t1)):
        total[:, k * rows : (k + 1) * rows] += lax.dot_general(
            w[...], t[...], BOTH_LAST, preferred_element_type=jnp.float32
        )

    @pl.when(step == pl.num_programs(0) - 1)
    def _():
        out_ref[...] = total[...].astype(out_ref.dtype)


def deep_product(w, t0, t1):
    m, depth = w.shape
    rows = t0.shape[0]
    block = divisor(depth, 3584)
    return pl.pallas_call(
        deep_kernel,
        grid=(depth // block,),
        in_specs=[pl.BlockSpec((m, block), lambda i: (0, i))] + [pl.BlockSpec((rows, block), lambda i: (0, i))] * 2,
        out_specs=pl.BlockSpec((m, 2 * rows), lambda i: (0, 0)),
        out_shape=jax.ShapeDtypeStruct((m, 2 * rows), jnp.bfloat16),
        scratch_shapes=[pltpu.VMEM((m, 2 * rows), jnp.float32)],
        compiler_params=pltpu.CompilerParams(vmem_limit_bytes=ROOM),
        cost_estimate=pl.CostEstimate(
            flops=4 * m * rows * depth, bytes_accessed=2 * depth * (m + 2 * rows), transcendentals=0
        ),
    )(*[pltpu.with_memory_space_constraint(x, pltpu.HBM) for x in (w, t0)], t1)


def product_kernel(n_w, n_t, cuts, first, rows, *refs):
    out_ref = refs[-1]
    for i, w in enumerate(refs[:n_w]):
        for k in range(n_t):
            total, start = 0.0, 0
            for t in refs[n_w + k * cuts : n_w + (k + 1) * cuts]:
                stop = start + t.shape[1]
                total += lax.dot_general(
                    w[:, start:stop], t[first : first + rows, :], BOTH_LAST, preferred_element_type=jnp.float32
                )
                start = stop
            out_ref[i, :, k * rows : (k + 1) * rows] = total.astype(out_ref.dtype)


def products(ws, ts, first, rows, dtype, after):
    m = ws[0].shape[0]
    shape = (len(ws), m, rows * len(ts))
    flat = [piece for t in ts for piece in t]
    return pl.pallas_call(
        functools.partial(product_kernel, len(ws), len(ts), len(ts[0]), first, rows),
        in_specs=[IN_VMEM] * (len(ws) + len(flat)) + [ANYWHERE] * len(after),
        out_specs=IN_VMEM,
        out_shape=jax.ShapeDtypeStruct(shape, dtype),
        compiler_params=pltpu.CompilerParams(vmem_limit_bytes=ROOM),
        cost_estimate=pl.CostEstimate(
            flops=len(ws) * m * rows, bytes_accessed=len(ws) * m * rows, transcendentals=0
        ),
    )(*ws, *flat, *after)


def join_kernel(places, *refs):
    n = len(places)
    part_refs, bias_ref, out_ref, joined = refs[:n], refs[n], refs[n + 1], refs[n + 2]
    me = lax.axis_index("row")
    for (j, token), part in zip(places, part_refs):
        m, rows = part.shape
        joined[pl.ds(pl.multiple_of((me ^ j) * m, 8), m), token : token + rows] = part[...].astype(jnp.float32)
    block = divisor(out_ref.shape[1], 512)
    for i in range(out_ref.shape[1] // block):
        cols = slice(i * block, (i + 1) * block)
        out_ref[:, cols] = (joined[cols, :].T + bias_ref[:, cols]).astype(out_ref.dtype)


def join(parts, rows, bias):
    width = bias.shape[0]
    return pl.pallas_call(
        functools.partial(join_kernel, [(j, token) for j, token, _ in parts]),
        out_shape=jax.ShapeDtypeStruct((rows, width), jnp.bfloat16),
        in_specs=[IN_VMEM] * (len(parts) + 1),
        out_specs=IN_VMEM,
        scratch_shapes=[pltpu.VMEM((width, rows), jnp.float32)],
        compiler_params=pltpu.CompilerParams(vmem_limit_bytes=ROOM),
        cost_estimate=pl.CostEstimate(flops=width * rows, bytes_accessed=4 * width * rows, transcendentals=0),
    )(*[part for _, _, part in parts], bias[None, :])


def shards(tokens, qkv_weight, qkv_bias):
    n_row, n_col = lax.axis_size("row"), lax.axis_size("col")
    planes = n_row // 2
    half, feats = tokens.shape
    weight = qkv_weight.reshape(feats, -1).T
    columns = weight.shape[0]

    def flip_col(x, j):
        return lax.ppermute(x, "col", [(i, i ^ j) for i in range(n_col)])

    def flip_row(x, j):
        return lax.ppermute(x, "row", [(i, i ^ j) for i in range(n_row)])

    (own,) = bands(tokens, [(0, 0, half)], n_col, [])
    js = list(range(n_col))
    (far,) = bands(weight, [(n_col - 1, 0, columns)], n_col, [own])
    near = bands(weight, [(j, 0, columns) for j in js[:-1]], n_col, [far])
    w_band = [near[0]] + [flip_col(x, j) for j, x in zip(js[1:], list(near[1:]) + [far])]
    here = deep_product(weight, tokens, flip_row(tokens, 1))
    here_other = flip_row(here[:, half:], 1)
    parts = [(0, 0, here[:, :half]), (1, 0, here_other)]

    held = []
    last = {0: own, 1: own}
    second = []
    for s in range(1, planes):
        if s == 2:
            last = dict(enumerate(passed([last[0], last[1]], [here_other, near[0]], SPACE)))
            held = [(last[i], came) for i, (_, came) in enumerate(held)]
        now = {}
        for parity in (0, 1):
            pairs, came = [], {}
            for p in range(parity, planes - 1, 2):
                if p - s + 1 >= 0:
                    pairs.append((p, p + 1))
                    came[p + 1] = p - s + 1
                if p + s < planes:
                    pairs.append((p + 1, p))
                    came[p] = p + s
            if pairs:
                now[parity] = lax.ppermute(
                    last[1 - parity], "row", [(2 * a + c, 2 * b + c) for a, b in pairs for c in (0, 1)]
                )
                held.append((now[parity], came))
                if s == 2:
                    second.append(now[parity])
        last = now

    def arrived(d, after, cuts):
        wanted = [next(i for i, (_, came) in enumerate(held) if came.get(p) == p ^ d) for p in range(planes)]
        used = sorted(set(wanted))
        value = list(choose([held[i][0] for i in used], [used.index(i) for i in wanted], after, cuts))
        return [value, [flip_row(x, 1) for x in value]]

    bits = [1 << b for b in range(n_col.bit_length() - 1)]
    groups = [[(d, 0, half) for d in range(1, planes - 1)], [(planes - 1, at, half // 2) for at in (0, half // 2)]]
    moved = w_band[1:]
    blocks = [None] + [arrived(d, second + moved, 2) for d in range(1, planes - 1)]
    after = [gate(moved + blocks[1][0] + blocks[1][1], GATE)]
    n_slot = 0
    came_back = []
    for n_group, group in enumerate(groups):
        if n_group:
            blocks.append(arrived(planes - 1, after + came_back, 1))
            after = [gate(blocks[planes - 1][1] + after, GATE2)]
        work = []
        for d, token, rows in group:
            turned = n_slot % len(bits)
            n_slot += 1
            order = bits[turned:] + bits[:turned]
            out = [j for j in js if j & order[0]]
            kept = [j for j in js if not j & order[0]]
            sent = products([w_band[j] for j in out], blocks[d], token, rows, jnp.bfloat16, after)
            after = [sent]
            came_back.append(flip_col(sent, order[0]))
            work.append([d, token, rows, order, kept, came_back[-1]])
        for item in work:
            d, token, rows, order, kept, got = item
            mine = products([w_band[j] for j in kept], blocks[d], token, rows, jnp.float32, after)
            after = [mine]
            item.append(mine)
        for d, token, rows, order, kept, got, mine in work:
            for n, bit in enumerate(order):
                if n:
                    got = flip_col(sent, bit)
                mine = mine + got.astype(jnp.float32)
                if n + 1 < len(order):
                    nxt = order[n + 1]
                    go = [i for i, j in enumerate(kept) if j & nxt]
                    stay = [i for i, j in enumerate(kept) if not j & nxt]
                    sent = jnp.stack([mine[i] for i in go]).astype(jnp.bfloat16)
                    mine = jnp.stack([mine[i] for i in stay])
                    kept = [kept[i] for i in stay]
            done = mine[0].astype(jnp.bfloat16)
            parts.append((2 * d, token, flip_row(done[:, :rows], 2 * d)))
            parts.append((2 * d + 1, token, flip_row(done[:, rows:], 2 * d + 1)))
    return join(parts, half, qkv_bias)


def solution(mesh):
    return jax.shard_map(
        shards,
        mesh=mesh,
        in_specs=(P("row", None), P(None, "col", "row", None), P("col")),
        out_specs=P("row", "col"),
        check_vma=False,
    )
```

```python
import functools

import jax
import jax.numpy as jnp
from jax import lax
from jax.experimental import pallas as pl
from jax.experimental.pallas import tpu as pltpu
from jax.sharding import PartitionSpec as P

ROOM = 14 * 1024 * 1024
SPACE = 0
KEPT = 4_000_000_000
BACKS = 9
IN_VMEM = pl.BlockSpec(memory_space=pltpu.VMEM)
IN_HBM = pl.BlockSpec(memory_space=pltpu.HBM)
ANYWHERE = pl.BlockSpec(memory_space=pl.ANY)
BOTH_LAST = (((1,), (1,)), ((), ()))


def divisor(size, most):
    return max(d for d in range(128, most + 1, 128) if size % d == 0)


def bands_kernel(pieces, n_col, n_x, *refs):
    outs, sems = refs[-1 - len(pieces) : -1], refs[-1]
    col = lax.axis_index("col")
    copies = []
    for i, (which, j, first, rows) in enumerate(pieces):
        band = refs[which].shape[1] // n_col
        start = pl.multiple_of((col ^ j) * band, 128)
        copies.append(
            pltpu.make_async_copy(refs[which].at[pl.ds(first, rows), pl.ds(start, band)], outs[i], sems.at[i])
        )
    for copy in copies:
        copy.start()
    for copy in copies:
        copy.wait()


def bands(xs, pieces, n_col, after):
    return pl.pallas_call(
        functools.partial(bands_kernel, pieces, n_col, len(xs)),
        out_shape=[
            jax.ShapeDtypeStruct((rows, xs[which].shape[1] // n_col), xs[which].dtype) for which, _, _, rows in pieces
        ],
        in_specs=[IN_HBM] * len(xs) + [ANYWHERE] * len(after),
        out_specs=[IN_VMEM] * len(pieces),
        scratch_shapes=[pltpu.SemaphoreType.DMA((len(pieces),))],
        compiler_params=pltpu.CompilerParams(vmem_limit_bytes=ROOM),
    )(*[pltpu.with_memory_space_constraint(x, pltpu.HBM) for x in xs], *after)


def choose_kernel(wanted, n, *refs):
    x_refs, outs, sem = refs[:n], refs[n:-1], refs[-1]
    plane = lax.axis_index("row") // 2
    for i, x in enumerate(x_refs):
        here = functools.reduce(jnp.logical_or, [plane == p for p, w in enumerate(wanted) if w == i])

        @pl.when(here)
        def _():
            first, copies = 0, []
            for k, out in enumerate(outs):
                width = out.shape[1]
                copies.append(pltpu.make_async_copy(x.at[:, pl.ds(first, width)], out, sem.at[k]))
                first += width
            for copy in copies:
                copy.start()
            for copy in copies:
                copy.wait()


def choose(xs, wanted, after, cuts):
    rows, width = xs[0].shape
    return pl.pallas_call(
        lambda *refs: choose_kernel(wanted, len(xs), *refs[: len(xs)], *refs[len(xs) + len(after) :]),
        out_shape=[jax.ShapeDtypeStruct((rows, width // cuts), xs[0].dtype)] * cuts,
        in_specs=[ANYWHERE] * (len(xs) + len(after)),
        out_specs=[IN_VMEM] * cuts,
        scratch_shapes=[pltpu.SemaphoreType.DMA((cuts,))],
        compiler_params=pltpu.CompilerParams(vmem_limit_bytes=ROOM),
    )(*xs, *after)


def pass_kernel(*refs):
    pass


def passed(xs, after, flops):
    return pl.pallas_call(
        pass_kernel,
        out_shape=[jax.ShapeDtypeStruct(x.shape, x.dtype) for x in xs],
        in_specs=[ANYWHERE] * (len(xs) + len(after)),
        out_specs=[ANYWHERE] * len(xs),
        input_output_aliases={i: i for i in range(len(xs))},
        compiler_params=pltpu.CompilerParams(vmem_limit_bytes=ROOM),
        cost_estimate=pl.CostEstimate(flops=flops, bytes_accessed=0, transcendentals=0),
    )(*xs, *after)


def gate_kernel(*refs):
    refs[-1][...] = jnp.zeros_like(refs[-1])


def gate(after, flops):
    return pl.pallas_call(
        gate_kernel,
        out_shape=jax.ShapeDtypeStruct((8, 128), jnp.float32),
        in_specs=[ANYWHERE] * len(after),
        out_specs=IN_VMEM,
        compiler_params=pltpu.CompilerParams(vmem_limit_bytes=ROOM),
        cost_estimate=pl.CostEstimate(flops=flops, bytes_accessed=0, transcendentals=0),
    )(*after)


def deep_kernel(w, t0, t1, out_ref, total):
    step = pl.program_id(0)

    @pl.when(step == 0)
    def _():
        total[...] = jnp.zeros_like(total)

    rows = t0.shape[0]
    for k, t in enumerate((t0, t1)):
        total[:, k * rows : (k + 1) * rows] += lax.dot_general(
            w[...], t[...], BOTH_LAST, preferred_element_type=jnp.float32
        )

    @pl.when(step == pl.num_programs(0) - 1)
    def _():
        out_ref[...] = total[...].astype(out_ref.dtype)


def deep_product(w, t0, t1):
    m, depth = w.shape
    rows = t0.shape[0]
    block = divisor(depth, 3584)
    return pl.pallas_call(
        deep_kernel,
        grid=(depth // block,),
        in_specs=[pl.BlockSpec((m, block), lambda i: (0, i))] + [pl.BlockSpec((rows, block), lambda i: (0, i))] * 2,
        out_specs=pl.BlockSpec((m, 2 * rows), lambda i: (0, 0)),
        out_shape=jax.ShapeDtypeStruct((m, 2 * rows), jnp.bfloat16),
        scratch_shapes=[pltpu.VMEM((m, 2 * rows), jnp.float32)],
        compiler_params=pltpu.CompilerParams(vmem_limit_bytes=ROOM),
        cost_estimate=pl.CostEstimate(
            flops=4 * m * rows * depth, bytes_accessed=2 * depth * (m + 2 * rows), transcendentals=0
        ),
    )(*[pltpu.with_memory_space_constraint(x, pltpu.HBM) for x in (w, t0)], t1)


def product_kernel(plan, n_in, *refs):
    outs = refs[len(refs) - len(plan) :]
    for out, (ws, ts) in zip(outs, plan):
        for i, w in enumerate(ws):
            for k, t in enumerate(ts):
                rows = refs[t].shape[0]
                out[i, :, k * rows : (k + 1) * rows] = lax.dot_general(
                    refs[w][...], refs[t][...], BOTH_LAST, preferred_element_type=jnp.float32
                ).astype(out.dtype)


def products(jobs, dtype, after, flops=0):
    arrays, plan, shapes = [], [], []
    for ws, ts in jobs:
        places = []
        for group in (ws, ts):
            place = []
            for x in group:
                known = [i for i, y in enumerate(arrays) if y is x]
                if not known:
                    arrays.append(x)
                place.append(known[0] if known else len(arrays) - 1)
            places.append(place)
        plan.append(tuple(places))
        shapes.append((len(ws), ws[0].shape[0], sum(t.shape[0] for t in ts)))
    size = sum(a * b * c for a, b, c in shapes)
    return pl.pallas_call(
        functools.partial(product_kernel, plan, len(arrays)),
        in_specs=[IN_VMEM] * len(arrays) + [ANYWHERE] * len(after),
        out_specs=[IN_VMEM] * len(jobs),
        out_shape=[jax.ShapeDtypeStruct(shape, dtype) for shape in shapes],
        compiler_params=pltpu.CompilerParams(vmem_limit_bytes=ROOM),
        cost_estimate=pl.CostEstimate(flops=flops + size, bytes_accessed=size, transcendentals=0),
    )(*arrays, *after)


def total_kernel(n_out, mine, got, *refs):
    outs = refs[-n_out:]
    rows = outs[0].shape[1]
    for k, out in enumerate(outs):
        part = slice(k * rows, (k + 1) * rows)
        out[...] = (mine[0, :, part] + got[0, :, part].astype(jnp.float32)).astype(out.dtype)


def totals(mine, got, rows, after):
    _, m, width = mine.shape
    return pl.pallas_call(
        functools.partial(total_kernel, width // rows),
        in_specs=[IN_VMEM] * 2 + [ANYWHERE] * len(after),
        out_specs=[IN_VMEM] * (width // rows),
        out_shape=[jax.ShapeDtypeStruct((m, rows), jnp.bfloat16)] * (width // rows),
        compiler_params=pltpu.CompilerParams(vmem_limit_bytes=ROOM),
        cost_estimate=pl.CostEstimate(flops=m * width, bytes_accessed=m * width, transcendentals=0),
    )(mine, got, *after)


def join_kernel(places, *refs):
    n = len(places)
    part_refs, bias_ref, out_ref, joined = refs[:n], refs[n], refs[n + 1], refs[n + 2]
    me = lax.axis_index("row")
    for (j, token), part in zip(places, part_refs):
        m, rows = part.shape
        joined[pl.ds(pl.multiple_of((me ^ j) * m, 8), m), token : token + rows] = part[...].astype(jnp.float32)
    block = divisor(out_ref.shape[1], 512)
    for i in range(out_ref.shape[1] // block):
        cols = slice(i * block, (i + 1) * block)
        out_ref[:, cols] = (joined[cols, :].T + bias_ref[:, cols]).astype(out_ref.dtype)


def join(parts, rows, bias):
    width = bias.shape[0]
    return pl.pallas_call(
        functools.partial(join_kernel, [(j, token) for j, token, _ in parts]),
        out_shape=jax.ShapeDtypeStruct((rows, width), jnp.bfloat16),
        in_specs=[IN_VMEM] * (len(parts) + 1),
        out_specs=IN_VMEM,
        scratch_shapes=[pltpu.VMEM((width, rows), jnp.float32)],
        compiler_params=pltpu.CompilerParams(vmem_limit_bytes=ROOM),
        cost_estimate=pl.CostEstimate(flops=width * rows, bytes_accessed=4 * width * rows, transcendentals=0),
    )(*[part for _, _, part in parts], bias[None, :])


def shards(tokens, qkv_weight, qkv_bias):
    n_row, n_col = lax.axis_size("row"), lax.axis_size("col")
    planes = n_row // 2
    half, feats = tokens.shape
    weight = qkv_weight.reshape(feats, -1).T
    columns = weight.shape[0]

    def flip_col(x, j):
        return lax.ppermute(x, "col", [(i, i ^ j) for i in range(n_col)])

    def flip_row(x, j):
        return lax.ppermute(x, "row", [(i, i ^ j) for i in range(n_row)])

    js = list(range(n_col))
    own, far = bands([tokens, weight], [(0, 0, 0, half), (1, n_col - 1, 0, columns)], n_col, [])
    near = bands([weight], [(0, j, 0, columns) for j in js[:-1]], n_col, [far])
    w_band = [near[0]] + [flip_col(x, j) for j, x in zip(js[1:], list(near[1:]) + [far])]
    here = deep_product(weight, tokens, flip_row(tokens, 1))
    here_other = flip_row(here[:, half:], 1)
    parts = [(0, 0, here[:, :half]), (1, 0, here_other)]

    held = []
    last = {0: own, 1: own}
    second = []
    for s in range(1, planes):
        if s == 2:
            last = dict(enumerate(passed([last[0], last[1]], [here_other, near[0]], SPACE)))
            held = [(last[i], came) for i, (_, came) in enumerate(held)]
        now = {}
        for parity in (0, 1):
            pairs, came = [], {}
            for p in range(parity, planes - 1, 2):
                if p - s + 1 >= 0:
                    pairs.append((p, p + 1))
                    came[p + 1] = p - s + 1
                if p + s < planes:
                    pairs.append((p + 1, p))
                    came[p] = p + s
            if pairs:
                now[parity] = lax.ppermute(
                    last[1 - parity], "row", [(2 * a + c, 2 * b + c) for a, b in pairs for c in (0, 1)]
                )
                held.append((now[parity], came))
                if s == 2:
                    second.append(now[parity])
        last = now

    def arrived(d, after):
        wanted = [next(i for i, (_, came) in enumerate(held) if came.get(p) == p ^ d) for p in range(planes)]
        used = sorted(set(wanted))
        (value,) = choose([held[i][0] for i in used], [used.index(i) for i in wanted], after, 1)
        return [value, flip_row(value, 1)]

    def halve(kept, mine, sums, orders):
        for bit in orders:
            mine = mine + sums.astype(jnp.float32)
            go = [i for i, j in enumerate(kept) if j & bit]
            stay = [i for i, j in enumerate(kept) if not j & bit]
            sent = jnp.stack([mine[i] for i in go]).astype(jnp.bfloat16)
            mine = jnp.stack([mine[i] for i in stay])
            kept = [kept[i] for i in stay]
            sums = flip_col(sent, bit)
        return mine, sums

    bits = [1 << b for b in range(n_col.bit_length() - 1)]
    orders = [bits[i % len(bits) :] + bits[: i % len(bits)] for i in range(planes + 1)]
    splits = [([j for j in js if j & o[0]], [j for j in js if not j & o[0]]) for o in orders]
    last_j = n_col - 1

    early = list(range(planes - 2, 0, -1))
    blocks = {d: arrived(d, second + [w_band[last_j]]) for d in early}
    firsts = products([([w_band[last_j]], blocks[d]) for d in early], jnp.bfloat16, [])
    got_first = [flip_col(x, orders[i][0]) for i, x in enumerate(firsts)]
    nexts = products(
        [([w_band[j] for j in splits[i][0] if j != last_j], blocks[d]) for i, d in enumerate(early)],
        jnp.bfloat16,
        list(firsts[:1]),
    )
    got_next = [flip_col(x, orders[i][0]) for i, x in enumerate(nexts)]
    mines = products(
        [([w_band[j] for j in splits[i][1]], blocks[d]) for i, d in enumerate(early)],
        jnp.float32,
        list(nexts[:1]) + got_first,
        KEPT,
    )
    def gather_sums(i, far, near):
        came = {last_j: far[0]}
        came.update(zip([j for j in splits[i][0] if j != last_j], near))
        return jnp.stack([came[j | orders[i][0]] for j in splits[i][1]])

    ended = []
    for i, d in enumerate(early):
        sums = gather_sums(i, got_first[i], got_next[i])
        ended.append(totals(*halve(splits[i][1], mines[i], sums, orders[i][1:]), half, []))
    swapped = [flip_row(other, 1) for _, other in ended[1:]]
    both = arrived(planes - 1, [x for pair in ended for x in pair])
    backs = []
    for i, d in enumerate(early):
        if i:
            back = flip_row(jnp.stack([ended[i][0], swapped[i - 1]]), 2 * d)
            backs.append(back)
            parts.append((2 * d + 1, 0, back[1]))
        else:
            back = flip_row(jnp.stack(ended[i]), 2 * d)
            hop = flip_row(jnp.concatenate([back[1], back[1][:, : half // 2]], axis=1), 1)
            parts.append((2 * d + 1, 0, hop[:, :half]))
        parts.append((2 * d, 0, back[0]))
    sents = list(mines[:1])
    late = []
    for core in (0, 1):
        i = len(early) + core
        near_js = [j for j in splits[i][0] if j != last_j]
        sents = products(
            [([w_band[last_j]], [both[core]]), ([w_band[j] for j in near_js], [both[core]])], jnp.bfloat16, sents[:1]
        )
        late.append((i, core, [flip_col(x, orders[i][0]) for x in sents]))
    late_mines = products(
        [([w_band[j] for j in splits[i][1]], [both[core]]) for i, core, _ in late], jnp.float32, sents[:1]
    )
    for (i, core, got), mine in zip(late, late_mines):
        (done,) = totals(
            *halve(splits[i][1], mine, gather_sums(i, *got), orders[i][1:]), half, backs[: BACKS * core]
        )
        parts.append((2 * (planes - 1) + core, 0, flip_row(done, 2 * (planes - 1) + core)))
    return join(parts, half, qkv_bias)


def solution(mesh):
    return jax.shard_map(
        shards,
        mesh=mesh,
        in_specs=(P("row", None), P(None, "col", "row", None), P("col")),
        out_specs=P("row", "col"),
        check_vma=False,
    )
```

```python
import functools

import jax
import jax.numpy as jnp
from jax import lax
from jax.experimental import pallas as pl
from jax.experimental.pallas import tpu as pltpu
from jax.sharding import PartitionSpec as P

ROOM = 14 * 1024 * 1024
KEPT = 4_000_000_000
BACKS = 0
IN_VMEM = pl.BlockSpec(memory_space=pltpu.VMEM)
IN_HBM = pl.BlockSpec(memory_space=pltpu.HBM)
ANYWHERE = pl.BlockSpec(memory_space=pl.ANY)
BOTH_LAST = (((1,), (1,)), ((), ()))


def divisor(size, most):
    return max(d for d in range(128, most + 1, 128) if size % d == 0)


def bands_kernel(pieces, n_col, n_x, *refs):
    outs, sems = refs[-1 - len(pieces) : -1], refs[-1]
    col = lax.axis_index("col")
    copies = []
    for i, (which, j, first, rows) in enumerate(pieces):
        band = refs[which].shape[1] // n_col
        start = pl.multiple_of((col ^ j) * band, 128)
        copies.append(
            pltpu.make_async_copy(refs[which].at[pl.ds(first, rows), pl.ds(start, band)], outs[i], sems.at[i])
        )
    for copy in copies:
        copy.start()
    for copy in copies:
        copy.wait()


def bands(xs, pieces, n_col, after):
    return pl.pallas_call(
        functools.partial(bands_kernel, pieces, n_col, len(xs)),
        out_shape=[
            jax.ShapeDtypeStruct((rows, xs[which].shape[1] // n_col), xs[which].dtype) for which, _, _, rows in pieces
        ],
        in_specs=[IN_HBM] * len(xs) + [ANYWHERE] * len(after),
        out_specs=[IN_VMEM] * len(pieces),
        scratch_shapes=[pltpu.SemaphoreType.DMA((len(pieces),))],
        compiler_params=pltpu.CompilerParams(vmem_limit_bytes=ROOM),
    )(*[pltpu.with_memory_space_constraint(x, pltpu.HBM) for x in xs], *after)


def choose_kernel(wanted, n, *refs):
    x_refs, outs, sem = refs[:n], refs[n:-1], refs[-1]
    plane = lax.axis_index("row") // 2
    for i, x in enumerate(x_refs):
        here = functools.reduce(jnp.logical_or, [plane == p for p, w in enumerate(wanted) if w == i])

        @pl.when(here)
        def _():
            first, copies = 0, []
            for k, out in enumerate(outs):
                width = out.shape[1]
                copies.append(pltpu.make_async_copy(x.at[:, pl.ds(first, width)], out, sem.at[k]))
                first += width
            for copy in copies:
                copy.start()
            for copy in copies:
                copy.wait()


def choose(xs, wanted, after, cuts):
    rows, width = xs[0].shape
    return pl.pallas_call(
        lambda *refs: choose_kernel(wanted, len(xs), *refs[: len(xs)], *refs[len(xs) + len(after) :]),
        out_shape=[jax.ShapeDtypeStruct((rows, width // cuts), xs[0].dtype)] * cuts,
        in_specs=[ANYWHERE] * (len(xs) + len(after)),
        out_specs=[IN_VMEM] * cuts,
        scratch_shapes=[pltpu.SemaphoreType.DMA((cuts,))],
        compiler_params=pltpu.CompilerParams(vmem_limit_bytes=ROOM),
    )(*xs, *after)


def pass_kernel(*refs):
    pass


def passed(xs, after):
    return pl.pallas_call(
        pass_kernel,
        out_shape=[jax.ShapeDtypeStruct(x.shape, x.dtype) for x in xs],
        in_specs=[ANYWHERE] * (len(xs) + len(after)),
        out_specs=[ANYWHERE] * len(xs),
        input_output_aliases={i: i for i in range(len(xs))},
        compiler_params=pltpu.CompilerParams(vmem_limit_bytes=ROOM),
    )(*xs, *after)


def gate_kernel(*refs):
    refs[-1][...] = jnp.zeros_like(refs[-1])


def gate(after, flops):
    return pl.pallas_call(
        gate_kernel,
        out_shape=jax.ShapeDtypeStruct((8, 128), jnp.float32),
        in_specs=[ANYWHERE] * len(after),
        out_specs=IN_VMEM,
        compiler_params=pltpu.CompilerParams(vmem_limit_bytes=ROOM),
        cost_estimate=pl.CostEstimate(flops=flops, bytes_accessed=0, transcendentals=0),
    )(*after)


def deep_kernel(w, t0, t1, out_ref, total):
    step = pl.program_id(0)

    @pl.when(step == 0)
    def _():
        total[...] = jnp.zeros_like(total)

    rows = t0.shape[0]
    for k, t in enumerate((t0, t1)):
        total[:, k * rows : (k + 1) * rows] += lax.dot_general(
            w[...], t[...], BOTH_LAST, preferred_element_type=jnp.float32
        )

    @pl.when(step == pl.num_programs(0) - 1)
    def _():
        out_ref[...] = total[...].astype(out_ref.dtype)


def deep_product(w, t0, t1):
    m, depth = w.shape
    rows = t0.shape[0]
    block = divisor(depth, 3584)
    return pl.pallas_call(
        deep_kernel,
        grid=(depth // block,),
        in_specs=[pl.BlockSpec((m, block), lambda i: (0, i))] + [pl.BlockSpec((rows, block), lambda i: (0, i))] * 2,
        out_specs=pl.BlockSpec((m, 2 * rows), lambda i: (0, 0)),
        out_shape=jax.ShapeDtypeStruct((m, 2 * rows), jnp.bfloat16),
        scratch_shapes=[pltpu.VMEM((m, 2 * rows), jnp.float32)],
        compiler_params=pltpu.CompilerParams(vmem_limit_bytes=ROOM),
        cost_estimate=pl.CostEstimate(
            flops=4 * m * rows * depth, bytes_accessed=2 * depth * (m + 2 * rows), transcendentals=0
        ),
    )(*[pltpu.with_memory_space_constraint(x, pltpu.HBM) for x in (w, t0)], t1)


def product_kernel(plan, n_in, *refs):
    outs = refs[len(refs) - len(plan) :]
    for out, (ws, ts) in zip(outs, plan):
        for i, w in enumerate(ws):
            for k, t in enumerate(ts):
                rows = refs[t].shape[0]
                out[i, :, k * rows : (k + 1) * rows] = lax.dot_general(
                    refs[w][...], refs[t][...], BOTH_LAST, preferred_element_type=jnp.float32
                ).astype(out.dtype)


def products(jobs, dtype, after, flops=0):
    arrays, plan, shapes = [], [], []
    for ws, ts in jobs:
        places = []
        for group in (ws, ts):
            place = []
            for x in group:
                known = [i for i, y in enumerate(arrays) if y is x]
                if not known:
                    arrays.append(x)
                place.append(known[0] if known else len(arrays) - 1)
            places.append(place)
        plan.append(tuple(places))
        shapes.append((len(ws), ws[0].shape[0], sum(t.shape[0] for t in ts)))
    size = sum(a * b * c for a, b, c in shapes)
    return pl.pallas_call(
        functools.partial(product_kernel, plan, len(arrays)),
        in_specs=[IN_VMEM] * len(arrays) + [ANYWHERE] * len(after),
        out_specs=[IN_VMEM] * len(jobs),
        out_shape=[jax.ShapeDtypeStruct(shape, dtype) for shape in shapes],
        compiler_params=pltpu.CompilerParams(vmem_limit_bytes=ROOM),
        cost_estimate=pl.CostEstimate(flops=flops + size, bytes_accessed=size, transcendentals=0),
    )(*arrays, *after)


def total_kernel(n_out, mine, got, *refs):
    outs = refs[-n_out:]
    rows = outs[0].shape[1]
    for k, out in enumerate(outs):
        part = slice(k * rows, (k + 1) * rows)
        out[...] = (mine[0, :, part] + got[0, :, part].astype(jnp.float32)).astype(out.dtype)


def totals(mine, got, rows, after):
    _, m, width = mine.shape
    return pl.pallas_call(
        functools.partial(total_kernel, width // rows),
        in_specs=[IN_VMEM] * 2 + [ANYWHERE] * len(after),
        out_specs=[IN_VMEM] * (width // rows),
        out_shape=[jax.ShapeDtypeStruct((m, rows), jnp.bfloat16)] * (width // rows),
        compiler_params=pltpu.CompilerParams(vmem_limit_bytes=ROOM),
        cost_estimate=pl.CostEstimate(flops=m * width, bytes_accessed=m * width, transcendentals=0),
    )(mine, got, *after)


def join_kernel(places, *refs):
    n = len(places)
    part_refs, bias_ref, out_ref, joined = refs[:n], refs[n], refs[n + 1], refs[n + 2]
    me = lax.axis_index("row")
    plane, core = me // 2, me % 2
    for (came, other), part in zip(places, part_refs):
        m = part.shape[0]
        source = functools.reduce(lambda x, p: jnp.where(plane == p, came[p], x), range(1, len(came)), came[0])
        start = pl.multiple_of((2 * source + (core ^ other)) * m, 8)
        joined[pl.ds(start, m), :] = part[...].astype(jnp.float32)
    block = divisor(out_ref.shape[1], 512)
    for i in range(out_ref.shape[1] // block):
        cols = slice(i * block, (i + 1) * block)
        out_ref[:, cols] = (joined[cols, :].T + bias_ref[:, cols]).astype(out_ref.dtype)


def join(parts, rows, bias):
    width = bias.shape[0]
    return pl.pallas_call(
        functools.partial(join_kernel, [(came, other) for came, other, _ in parts]),
        out_shape=jax.ShapeDtypeStruct((rows, width), jnp.bfloat16),
        in_specs=[IN_VMEM] * (len(parts) + 1),
        out_specs=IN_VMEM,
        scratch_shapes=[pltpu.VMEM((width, rows), jnp.float32)],
        compiler_params=pltpu.CompilerParams(vmem_limit_bytes=ROOM),
        cost_estimate=pl.CostEstimate(flops=width * rows, bytes_accessed=4 * width * rows, transcendentals=0),
    )(*[part for _, _, part in parts], bias[None, :])


def chain(own, planes, send, after):
    held = []
    last = {0: own, 1: own}
    second = []
    for s in range(1, planes):
        if s == 2:
            last = dict(enumerate(passed([last[0], last[1]], after)))
            held = [(last[i], came) for i, (_, came) in enumerate(held)]
        now = {}
        for parity in (0, 1):
            pairs, came = [], {}
            for p in range(parity, planes - 1, 2):
                if p - s + 1 >= 0:
                    pairs.append((p, p + 1))
                    came[p + 1] = p - s + 1
                if p + s < planes:
                    pairs.append((p + 1, p))
                    came[p] = p + s
            if pairs:
                now[parity] = send(last[1 - parity], pairs)
                held.append((now[parity], came))
                if s == 2:
                    second.append(now[parity])
        last = now
    slots = []
    for d in range(planes - 2, 0, -1) if planes > 2 else ():
        slots.append(d)
    found = []
    for d in slots + [planes - 1]:
        wanted = [next(i for i, (_, came) in enumerate(held) if came.get(p) == p ^ d) for p in range(planes)]
        used = sorted(set(wanted))
        found.append(([held[i][0] for i in used], [used.index(i) for i in wanted], [p ^ d for p in range(planes)]))
    return found, second


def line_of_four(own, send, after):
    ends = [0, 1, 1, 0]
    swap = [(0, 1), (1, 0), (2, 3), (3, 2)]
    cross = send(own, [(0, 3), (3, 0)])
    (out,) = choose([cross, own], ends, after, 1)
    near = send(out, swap)
    inner = send(out, [(1, 2), (2, 1)])
    (out,) = choose([own, inner], ends, [near], 1)
    final = send(out, swap)
    slots = [
        ([cross, inner], ends, [3, 2, 1, 0]),
        ([near], [0, 0, 0, 0], [1, 3, 0, 2]),
        ([final], [0, 0, 0, 0], [2, 0, 3, 1]),
    ]
    return slots, [near, inner]


def shards(tokens, qkv_weight, qkv_bias):
    n_row, n_col = lax.axis_size("row"), lax.axis_size("col")
    planes = n_row // 2
    half, feats = tokens.shape
    weight = qkv_weight.reshape(feats, -1).T
    columns = weight.shape[0]

    def flip_col(x, j):
        return lax.ppermute(x, "col", [(i, i ^ j) for i in range(n_col)])

    def flip_row(x, j):
        return lax.ppermute(x, "row", [(i, i ^ j) for i in range(n_row)])

    js = list(range(n_col))
    own, far = bands([tokens, weight], [(0, 0, 0, half), (1, n_col - 1, 0, columns)], n_col, [])
    near = bands([weight], [(0, j, 0, columns) for j in js[:-1]], n_col, [far])
    w_band = [near[0]] + [flip_col(x, j) for j, x in zip(js[1:], list(near[1:]) + [far])]
    here = deep_product(weight, tokens, flip_row(tokens, 1))
    here_other = flip_row(here[:, half:], 1)
    everyone = list(range(planes))
    parts = [(everyone, 0, here[:, :half]), (everyone, 1, here_other)]

    def send(x, pairs):
        return lax.ppermute(x, "row", [(2 * a + c, 2 * b + c) for a, b in pairs for c in (0, 1)])

    if planes == 4:
        slots, second = line_of_four(own, send, [here_other, near[0]])
    else:
        slots, second = chain(own, planes, send, [here_other, near[0]])

    def arrived(slot, after):
        arrays, wanted, _ = slot
        (value,) = choose(arrays, wanted, after, 1)
        return [value, flip_row(value, 1)]

    def halve(kept, mine, sums, orders):
        for bit in orders:
            mine = mine + sums.astype(jnp.float32)
            go = [i for i, j in enumerate(kept) if j & bit]
            stay = [i for i, j in enumerate(kept) if not j & bit]
            sent = jnp.stack([mine[i] for i in go]).astype(jnp.bfloat16)
            mine = jnp.stack([mine[i] for i in stay])
            kept = [kept[i] for i in stay]
            sums = flip_col(sent, bit)
        return mine, sums

    bits = [1 << b for b in range(n_col.bit_length() - 1)]
    orders = [bits[i % len(bits) :] + bits[: i % len(bits)] for i in range(planes + 1)]
    splits = [([j for j in js if j & o[0]], [j for j in js if not j & o[0]]) for o in orders]
    last_j = n_col - 1

    early = list(range(planes - 2))
    blocks = {d: arrived(slots[d], second + [w_band[last_j]]) for d in early}
    firsts = products([([w_band[last_j]], blocks[d]) for d in early], jnp.bfloat16, [])
    got_first = [flip_col(x, orders[i][0]) for i, x in enumerate(firsts)]
    nexts = products(
        [([w_band[j] for j in splits[i][0] if j != last_j], blocks[d]) for i, d in enumerate(early)],
        jnp.bfloat16,
        list(firsts[:1]),
    )
    got_next = [flip_col(x, orders[i][0]) for i, x in enumerate(nexts)]
    mines = products(
        [([w_band[j] for j in splits[i][1]], blocks[d]) for i, d in enumerate(early)],
        jnp.float32,
        list(nexts[:1]) + got_first,
        KEPT,
    )
    def gather_sums(i, far, near):
        came = {last_j: far[0]}
        came.update(zip([j for j in splits[i][0] if j != last_j], near))
        return jnp.stack([came[j | orders[i][0]] for j in splits[i][1]])

    ended = []
    for i, d in enumerate(early):
        sums = gather_sums(i, got_first[i], got_next[i])
        ended.append(totals(*halve(splits[i][1], mines[i], sums, orders[i][1:]), half, []))
    swapped = [flip_row(other, 1) for _, other in ended[1:]]
    both = arrived(slots[-1], [x for pair in ended for x in pair])
    backs = []
    for i, slot in enumerate(slots[:-1]):
        home = [(p, c) for p, c in enumerate(slot[2])]
        source = [slot[2].index(c) for c in everyone]
        if i:
            back = send(jnp.stack([ended[i][0], swapped[i - 1]]), home)
            backs.append(back)
            parts.append((source, 1, back[1]))
        else:
            back = send(jnp.stack(ended[i]), home)
            hop = flip_row(jnp.concatenate([back[1], back[1][:, : half // 2]], axis=1), 1)
            parts.append((source, 1, hop[:, :half]))
        parts.append((source, 0, back[0]))
    sents = list(mines[:1])
    late = []
    for core in (0, 1):
        i = len(early) + core
        near_js = [j for j in splits[i][0] if j != last_j]
        sents = products(
            [([w_band[last_j]], [both[core]]), ([w_band[j] for j in near_js], [both[core]])], jnp.bfloat16, sents[:1]
        )
        late.append((i, core, [flip_col(x, orders[i][0]) for x in sents]))
    late_mines = products(
        [([w_band[j] for j in splits[i][1]], [both[core]]) for i, core, _ in late], jnp.float32, sents[:1]
    )
    for (i, core, got), mine in zip(late, late_mines):
        (done,) = totals(
            *halve(splits[i][1], mine, gather_sums(i, *got), orders[i][1:]), half, backs[: BACKS * core]
        )
        home = [(2 * p + c, 2 * q + (c ^ core)) for p, q in enumerate(slots[-1][2]) for c in (0, 1)]
        source = [slots[-1][2].index(q) for q in everyone]
        parts.append((source, core, lax.ppermute(done, "row", home)))
    return join(parts, half, qkv_bias)


def solution(mesh):
    return jax.shard_map(
        shards,
        mesh=mesh,
        in_specs=(P("row", None), P(None, "col", "row", None), P("col")),
        out_specs=P("row", "col"),
        check_vma=False,
    )
```

```python
import functools

import jax
import jax.numpy as jnp
from jax import lax
from jax.experimental import pallas as pl
from jax.experimental.pallas import tpu as pltpu
from jax.sharding import PartitionSpec as P

ROOM = 14 * 1024 * 1024
KEPT = 0
BACKS = 0
IN_VMEM = pl.BlockSpec(memory_space=pltpu.VMEM)
IN_HBM = pl.BlockSpec(memory_space=pltpu.HBM)
ANYWHERE = pl.BlockSpec(memory_space=pl.ANY)
BOTH_LAST = (((1,), (1,)), ((), ()))


def divisor(size, most):
    return max(d for d in range(128, most + 1, 128) if size % d == 0)


def bands_kernel(pieces, n_col, n_x, *refs):
    outs, sems = refs[-1 - len(pieces) : -1], refs[-1]
    col = lax.axis_index("col")
    copies = []
    for i, (which, j, first, rows) in enumerate(pieces):
        band = refs[which].shape[1] // n_col
        start = pl.multiple_of((col ^ j) * band, 128)
        copies.append(
            pltpu.make_async_copy(refs[which].at[pl.ds(first, rows), pl.ds(start, band)], outs[i], sems.at[i])
        )
    for copy in copies:
        copy.start()
    for copy in copies:
        copy.wait()


def bands(xs, pieces, n_col, after):
    return pl.pallas_call(
        functools.partial(bands_kernel, pieces, n_col, len(xs)),
        out_shape=[
            jax.ShapeDtypeStruct((rows, xs[which].shape[1] // n_col), xs[which].dtype) for which, _, _, rows in pieces
        ],
        in_specs=[IN_HBM] * len(xs) + [ANYWHERE] * len(after),
        out_specs=[IN_VMEM] * len(pieces),
        scratch_shapes=[pltpu.SemaphoreType.DMA((len(pieces),))],
        compiler_params=pltpu.CompilerParams(vmem_limit_bytes=ROOM),
    )(*[pltpu.with_memory_space_constraint(x, pltpu.HBM) for x in xs], *after)


def choose_kernel(wanted, n, *refs):
    x_refs, outs, sem = refs[:n], refs[n:-1], refs[-1]
    plane = lax.axis_index("row") // 2
    for i, x in enumerate(x_refs):
        here = functools.reduce(jnp.logical_or, [plane == p for p, w in enumerate(wanted) if w == i])

        @pl.when(here)
        def _():
            first, copies = 0, []
            for k, out in enumerate(outs):
                width = out.shape[1]
                copies.append(pltpu.make_async_copy(x.at[:, pl.ds(first, width)], out, sem.at[k]))
                first += width
            for copy in copies:
                copy.start()
            for copy in copies:
                copy.wait()


def choose(xs, wanted, after, cuts):
    rows, width = xs[0].shape
    return pl.pallas_call(
        lambda *refs: choose_kernel(wanted, len(xs), *refs[: len(xs)], *refs[len(xs) + len(after) :]),
        out_shape=[jax.ShapeDtypeStruct((rows, width // cuts), xs[0].dtype)] * cuts,
        in_specs=[ANYWHERE] * (len(xs) + len(after)),
        out_specs=[IN_VMEM] * cuts,
        scratch_shapes=[pltpu.SemaphoreType.DMA((cuts,))],
        compiler_params=pltpu.CompilerParams(vmem_limit_bytes=ROOM),
    )(*xs, *after)


def pass_kernel(*refs):
    pass


def passed(xs, after):
    return pl.pallas_call(
        pass_kernel,
        out_shape=[jax.ShapeDtypeStruct(x.shape, x.dtype) for x in xs],
        in_specs=[ANYWHERE] * (len(xs) + len(after)),
        out_specs=[ANYWHERE] * len(xs),
        input_output_aliases={i: i for i in range(len(xs))},
        compiler_params=pltpu.CompilerParams(vmem_limit_bytes=ROOM),
    )(*xs, *after)


def gate_kernel(*refs):
    refs[-1][...] = jnp.zeros_like(refs[-1])


def gate(after, flops):
    return pl.pallas_call(
        gate_kernel,
        out_shape=jax.ShapeDtypeStruct((8, 128), jnp.float32),
        in_specs=[ANYWHERE] * len(after),
        out_specs=IN_VMEM,
        compiler_params=pltpu.CompilerParams(vmem_limit_bytes=ROOM),
        cost_estimate=pl.CostEstimate(flops=flops, bytes_accessed=0, transcendentals=0),
    )(*after)


def deep_kernel(w, t0, t1, out_ref, total):
    step = pl.program_id(0)

    @pl.when(step == 0)
    def _():
        total[...] = jnp.zeros_like(total)

    rows = t0.shape[0]
    for k, t in enumerate((t0, t1)):
        total[:, k * rows : (k + 1) * rows] += lax.dot_general(
            w[...], t[...], BOTH_LAST, preferred_element_type=jnp.float32
        )

    @pl.when(step == pl.num_programs(0) - 1)
    def _():
        out_ref[...] = total[...].astype(out_ref.dtype)


def deep_product(w, t0, t1):
    m, depth = w.shape
    rows = t0.shape[0]
    block = divisor(depth, 3584)
    return pl.pallas_call(
        deep_kernel,
        grid=(depth // block,),
        in_specs=[pl.BlockSpec((m, block), lambda i: (0, i))] + [pl.BlockSpec((rows, block), lambda i: (0, i))] * 2,
        out_specs=pl.BlockSpec((m, 2 * rows), lambda i: (0, 0)),
        out_shape=jax.ShapeDtypeStruct((m, 2 * rows), jnp.bfloat16),
        scratch_shapes=[pltpu.VMEM((m, 2 * rows), jnp.float32)],
        compiler_params=pltpu.CompilerParams(vmem_limit_bytes=ROOM),
        cost_estimate=pl.CostEstimate(
            flops=4 * m * rows * depth, bytes_accessed=2 * depth * (m + 2 * rows), transcendentals=0
        ),
    )(*[pltpu.with_memory_space_constraint(x, pltpu.HBM) for x in (w, t0)], t1)


def product_kernel(plan, n_in, *refs):
    outs = refs[len(refs) - len(plan) :]
    for out, (ws, ts) in zip(outs, plan):
        for i, w in enumerate(ws):
            for k, t in enumerate(ts):
                rows = refs[t].shape[0]
                out[i, :, k * rows : (k + 1) * rows] = lax.dot_general(
                    refs[w][...], refs[t][...], BOTH_LAST, preferred_element_type=jnp.float32
                ).astype(out.dtype)


def products(jobs, dtype, after, flops=0):
    arrays, plan, shapes = [], [], []
    for ws, ts in jobs:
        places = []
        for group in (ws, ts):
            place = []
            for x in group:
                known = [i for i, y in enumerate(arrays) if y is x]
                if not known:
                    arrays.append(x)
                place.append(known[0] if known else len(arrays) - 1)
            places.append(place)
        plan.append(tuple(places))
        shapes.append((len(ws), ws[0].shape[0], sum(t.shape[0] for t in ts)))
    size = sum(a * b * c for a, b, c in shapes)
    return pl.pallas_call(
        functools.partial(product_kernel, plan, len(arrays)),
        in_specs=[IN_VMEM] * len(arrays) + [ANYWHERE] * len(after),
        out_specs=[IN_VMEM] * len(jobs),
        out_shape=[jax.ShapeDtypeStruct(shape, dtype) for shape in shapes],
        compiler_params=pltpu.CompilerParams(vmem_limit_bytes=ROOM),
        cost_estimate=pl.CostEstimate(flops=flops + size, bytes_accessed=size, transcendentals=0),
    )(*arrays, *after)


def add_kernel(n, *refs):
    out = refs[-1]
    for i in range(n):
        out[i : i + 1] = (refs[i][...] + refs[n + i][...].astype(jnp.float32)).astype(out.dtype)


def added(mine, came, dtype):
    shape = (len(mine), *mine[0].shape[1:])
    size = shape[0] * shape[1] * shape[2]
    return pl.pallas_call(
        functools.partial(add_kernel, len(mine)),
        in_specs=[IN_VMEM] * (2 * len(mine)),
        out_specs=IN_VMEM,
        out_shape=jax.ShapeDtypeStruct(shape, dtype),
        compiler_params=pltpu.CompilerParams(vmem_limit_bytes=ROOM),
        cost_estimate=pl.CostEstimate(flops=size, bytes_accessed=size, transcendentals=0),
    )(*mine, *came)


def total_kernel(n_out, n_terms, *refs):
    outs = refs[-n_out:]
    rows = outs[0].shape[1]
    for k, out in enumerate(outs):
        part = slice(k * rows, (k + 1) * rows)
        total = refs[0][0, :, part]
        for term in refs[1:n_terms]:
            total = total + term[0, :, part].astype(jnp.float32)
        out[...] = total.astype(out.dtype)


def totals(terms, rows, after):
    _, m, width = terms[0].shape
    return pl.pallas_call(
        functools.partial(total_kernel, width // rows, len(terms)),
        in_specs=[IN_VMEM] * len(terms) + [ANYWHERE] * len(after),
        out_specs=[IN_VMEM] * (width // rows),
        out_shape=[jax.ShapeDtypeStruct((m, rows), jnp.bfloat16)] * (width // rows),
        compiler_params=pltpu.CompilerParams(vmem_limit_bytes=ROOM),
        cost_estimate=pl.CostEstimate(flops=m * width, bytes_accessed=m * width, transcendentals=0),
    )(*terms, *after)


def join_kernel(places, *refs):
    n = len(places)
    part_refs, bias_ref, out_ref, joined = refs[:n], refs[n], refs[n + 1], refs[n + 2]
    me = lax.axis_index("row")
    plane, core = me // 2, me % 2
    for (came, other), part in zip(places, part_refs):
        m = part.shape[0]
        source = functools.reduce(lambda x, p: jnp.where(plane == p, came[p], x), range(1, len(came)), came[0])
        start = pl.multiple_of((2 * source + (core ^ other)) * m, 8)
        joined[pl.ds(start, m), :] = part[...].astype(jnp.float32)
    block = divisor(out_ref.shape[1], 512)
    for i in range(out_ref.shape[1] // block):
        cols = slice(i * block, (i + 1) * block)
        out_ref[:, cols] = (joined[cols, :].T + bias_ref[:, cols]).astype(out_ref.dtype)


def join(parts, rows, bias):
    width = bias.shape[0]
    return pl.pallas_call(
        functools.partial(join_kernel, [(came, other) for came, other, _ in parts]),
        out_shape=jax.ShapeDtypeStruct((rows, width), jnp.bfloat16),
        in_specs=[IN_VMEM] * (len(parts) + 1),
        out_specs=IN_VMEM,
        scratch_shapes=[pltpu.VMEM((width, rows), jnp.float32)],
        compiler_params=pltpu.CompilerParams(vmem_limit_bytes=ROOM),
        cost_estimate=pl.CostEstimate(flops=width * rows, bytes_accessed=4 * width * rows, transcendentals=0),
    )(*[part for _, _, part in parts], bias[None, :])


def chain(own, planes, send, after):
    held = []
    last = {0: own, 1: own}
    second = []
    for s in range(1, planes):
        if s == 2:
            last = dict(enumerate(passed([last[0], last[1]], after)))
            held = [(last[i], came) for i, (_, came) in enumerate(held)]
        now = {}
        for parity in (0, 1):
            pairs, came = [], {}
            for p in range(parity, planes - 1, 2):
                if p - s + 1 >= 0:
                    pairs.append((p, p + 1))
                    came[p + 1] = p - s + 1
                if p + s < planes:
                    pairs.append((p + 1, p))
                    came[p] = p + s
            if pairs:
                now[parity] = send(last[1 - parity], pairs)
                held.append((now[parity], came))
                if s == 2:
                    second.append(now[parity])
        last = now
    slots = []
    for d in range(planes - 2, 0, -1) if planes > 2 else ():
        slots.append(d)
    found = []
    for d in slots + [planes - 1]:
        wanted = [next(i for i, (_, came) in enumerate(held) if came.get(p) == p ^ d) for p in range(planes)]
        used = sorted(set(wanted))
        found.append(([held[i][0] for i in used], [used.index(i) for i in wanted], [p ^ d for p in range(planes)]))
    return found, second


def line_of_four(own, send, after):
    ends = [0, 1, 1, 0]
    swap = [(0, 1), (1, 0), (2, 3), (3, 2)]
    cross = send(own, [(0, 3), (3, 0)])
    (out,) = choose([cross, own], ends, after, 1)
    near = send(out, swap)
    inner = send(out, [(1, 2), (2, 1)])
    (out,) = choose([own, inner], ends, [near], 1)
    final = send(out, swap)
    slots = [
        ([cross, inner], ends, [3, 2, 1, 0]),
        ([near], [0, 0, 0, 0], [1, 3, 0, 2]),
        ([final], [0, 0, 0, 0], [2, 0, 3, 1]),
    ]
    return slots, [near, inner]


def shards(tokens, qkv_weight, qkv_bias):
    n_row, n_col = lax.axis_size("row"), lax.axis_size("col")
    planes = n_row // 2
    half, feats = tokens.shape
    weight = qkv_weight.reshape(feats, -1).T
    columns = weight.shape[0]

    def flip_col(x, j):
        return lax.ppermute(x, "col", [(i, i ^ j) for i in range(n_col)])

    def flip_row(x, j):
        return lax.ppermute(x, "row", [(i, i ^ j) for i in range(n_row)])

    js = list(range(n_col))
    own, far = bands([tokens, weight], [(0, 0, 0, half), (1, n_col - 1, 0, columns)], n_col, [])
    near = bands([weight], [(0, j, 0, columns) for j in js[:-1]], n_col, [far])
    w_band = [near[0]] + [flip_col(x, j) for j, x in zip(js[1:], list(near[1:]) + [far])]
    here = deep_product(weight, tokens, flip_row(tokens, 1))
    here_other = flip_row(here[:, half:], 1)
    everyone = list(range(planes))
    parts = [(everyone, 0, here[:, :half]), (everyone, 1, here_other)]

    def send(x, pairs):
        return lax.ppermute(x, "row", [(2 * a + c, 2 * b + c) for a, b in pairs for c in (0, 1)])

    if planes == 4:
        slots, second = line_of_four(own, send, [here_other, near[0]])
    else:
        slots, second = chain(own, planes, send, [here_other, near[0]])

    def arrived(slot, after):
        arrays, wanted, _ = slot
        (value,) = choose(arrays, wanted, after, 1)
        return [value, flip_row(value, 1)]

    def apart(x):
        return [x] if x.shape[0] == 1 else [x[i : i + 1] for i in range(x.shape[0])]

    def halve(kept, mine, came, orders):
        for n, bit in enumerate(orders):
            go = [i for i, j in enumerate(kept) if j & bit]
            stay = [i for i, j in enumerate(kept) if not j & bit]
            got = flip_col(added([mine[i] for i in go], [came[i] for i in go], jnp.bfloat16), bit)
            kept = [kept[i] for i in stay]
            if n + 1 == len(orders):
                return [mine[stay[0]], came[stay[0]], got]
            mine = [added([mine[i]], [came[i]], jnp.float32) for i in stay]
            came = apart(got)
        return [mine[0], came[0]]

    bits = [1 << b for b in range(n_col.bit_length() - 1)]
    orders = [bits[i % len(bits) :] + bits[: i % len(bits)] for i in range(planes + 1)]
    splits = [([j for j in js if j & o[0]], [j for j in js if not j & o[0]]) for o in orders]
    last_j = n_col - 1

    early = list(range(planes - 2))
    blocks = {d: arrived(slots[d], second + [w_band[last_j]]) for d in early}
    firsts = products([([w_band[last_j]], blocks[d]) for d in early], jnp.bfloat16, [])
    got_first = [flip_col(x, orders[i][0]) for i, x in enumerate(firsts)]
    nexts = products(
        [([w_band[j] for j in splits[i][0] if j != last_j], blocks[d]) for i, d in enumerate(early)],
        jnp.bfloat16,
        list(firsts[:1]),
    )
    got_next = [flip_col(x, orders[i][0]) for i, x in enumerate(nexts)]
    passing = [[j for j in splits[i][1] if len(orders[i]) > 1 and j & orders[i][1]] for i in early]
    staying = [[j for j in splits[i][1] if j not in passing[i]] for i in early]
    mine_of, first_mine = {}, list(nexts[:1])
    for which, flops in ((passing, KEPT), (staying, 0)):
        mines = products(
            [([w_band[j]], blocks[d]) for i, d in enumerate(early) for j in which[i]], jnp.float32, first_mine, flops
        )
        first_mine = list(mines[:1])
        mine_of.update(zip([(i, j) for i in early for j in which[i]], mines))

    def gather_sums(i, far, near):
        came = {last_j: far}
        came.update(zip([j for j in splits[i][0] if j != last_j], apart(near)))
        return [came[j | orders[i][0]] for j in splits[i][1]]

    n_kept = n_col // 2
    ended = []
    for i, d in enumerate(early):
        sums = gather_sums(i, got_first[i], got_next[i])
        ended.append(totals(halve(splits[i][1], [mine_of[i, j] for j in splits[i][1]], sums, orders[i][1:]), half, []))
    swapped = [flip_row(other, 1) for _, other in ended[1:]]
    both = arrived(slots[-1], [x for pair in ended for x in pair])
    backs = []
    for i, slot in enumerate(slots[:-1]):
        home = [(p, c) for p, c in enumerate(slot[2])]
        source = [slot[2].index(c) for c in everyone]
        if i:
            back = send(jnp.stack([ended[i][0], swapped[i - 1]]), home)
            backs.append(back)
            parts.append((source, 1, back[1]))
        else:
            back = send(jnp.stack(ended[i]), home)
            hop = flip_row(jnp.concatenate([back[1], back[1][:, : half // 2]], axis=1), 1)
            parts.append((source, 1, hop[:, :half]))
        parts.append((source, 0, back[0]))
    sents = first_mine
    late = []
    for core in (0, 1):
        i = len(early) + core
        near_js = [j for j in splits[i][0] if j != last_j]
        sents = products(
            [([w_band[last_j]], [both[core]]), ([w_band[j] for j in near_js], [both[core]])], jnp.bfloat16, sents[:1]
        )
        late.append((i, core, [flip_col(x, orders[i][0]) for x in sents]))
    late_mines = products(
        [([w_band[j]], [both[core]]) for i, core, _ in late for j in splits[i][1]], jnp.float32, list(sents[:1])
    )
    for i, core, got in late:
        mine = late_mines[core * n_kept : (core + 1) * n_kept]
        (done,) = totals(halve(splits[i][1], mine, gather_sums(i, *got), orders[i][1:]), half, [])
        home = [(2 * p + c, 2 * q + (c ^ core)) for p, q in enumerate(slots[-1][2]) for c in (0, 1)]
        source = [slots[-1][2].index(q) for q in everyone]
        parts.append((source, core, lax.ppermute(done, "row", home)))
    return join(parts, half, qkv_bias)


def solution(mesh):
    return jax.shard_map(
        shards,
        mesh=mesh,
        in_specs=(P("row", None), P(None, "col", "row", None), P("col")),
        out_specs=P("row", "col"),
        check_vma=False,
    )
```

```python
import functools

import jax
import jax.numpy as jnp
from jax import lax
from jax.experimental import pallas as pl
from jax.experimental.pallas import tpu as pltpu
from jax.sharding import PartitionSpec as P

ROOM = 14 * 1024 * 1024
KEPT = 0
BACKS = 0
CUTS = 1
XCUTS = 2
IN_VMEM = pl.BlockSpec(memory_space=pltpu.VMEM)
IN_HBM = pl.BlockSpec(memory_space=pltpu.HBM)
ANYWHERE = pl.BlockSpec(memory_space=pl.ANY)
BOTH_LAST = (((1,), (1,)), ((), ()))


def divisor(size, most):
    return max(d for d in range(128, most + 1, 128) if size % d == 0)


def bands_kernel(pieces, n_col, *refs):
    outs, sems = refs[-1 - len(pieces) : -1], refs[-1]
    col = lax.axis_index("col")
    copies = []
    for i, (which, j, part) in enumerate(pieces):
        band, width = refs[which].shape[1] // n_col, outs[i].shape[1]
        start = pl.multiple_of((col ^ j) * band + part * width, 128)
        copies.append(pltpu.make_async_copy(refs[which].at[:, pl.ds(start, width)], outs[i], sems.at[i]))
    for copy in copies:
        copy.start()
    for copy in copies:
        copy.wait()


def bands(xs, pieces, n_col, after):
    shapes = [(xs[which].shape[0], xs[which].shape[1] // n_col // parts) for which, _, _, parts in pieces]
    return pl.pallas_call(
        functools.partial(bands_kernel, [piece[:3] for piece in pieces], n_col),
        out_shape=[jax.ShapeDtypeStruct(shape, xs[piece[0]].dtype) for shape, piece in zip(shapes, pieces)],
        in_specs=[IN_HBM] * len(xs) + [ANYWHERE] * len(after),
        out_specs=[IN_VMEM] * len(pieces),
        scratch_shapes=[pltpu.SemaphoreType.DMA((len(pieces),))],
        compiler_params=pltpu.CompilerParams(vmem_limit_bytes=ROOM),
    )(*[pltpu.with_memory_space_constraint(x, pltpu.HBM) for x in xs], *after)


def choose_kernel(wanted, counts, cuts, *refs):
    outs, sem = refs[-1 - cuts : -1], refs[-1]
    plane = lax.axis_index("row") // 2
    at = 0
    for i, count in enumerate(counts):
        pieces = refs[at : at + count]
        at += count
        here = functools.reduce(jnp.logical_or, [plane == p for p, w in enumerate(wanted) if w == i])

        @pl.when(here)
        def _():
            n = max(count, cuts)
            width = pieces[0].shape[1] * count // n
            copies = []
            for k in range(n):
                source, from_col = k * count // n, k * width % pieces[0].shape[1]
                target, to_col = k * cuts // n, k * width % outs[0].shape[1]
                copies.append(
                    pltpu.make_async_copy(
                        pieces[source].at[:, pl.ds(from_col, width)], outs[target].at[:, pl.ds(to_col, width)], sem.at[k]
                    )
                )
            for copy in copies:
                copy.start()
            for copy in copies:
                copy.wait()


def choose(xs, wanted, after, cuts=1):
    flat = [piece for x in xs for piece in x]
    counts = [len(x) for x in xs]
    shape = (flat[0].shape[0], sum(piece.shape[1] for piece in xs[0]) // cuts)
    return pl.pallas_call(
        lambda *refs: choose_kernel(wanted, counts, cuts, *refs[: len(flat)], *refs[len(flat) + len(after) :]),
        out_shape=[jax.ShapeDtypeStruct(shape, flat[0].dtype)] * cuts,
        in_specs=[ANYWHERE] * (len(flat) + len(after)),
        out_specs=[IN_VMEM] * cuts,
        scratch_shapes=[pltpu.SemaphoreType.DMA((max(counts + [cuts]),))],
        compiler_params=pltpu.CompilerParams(vmem_limit_bytes=ROOM),
    )(*flat, *after)


def pass_kernel(*refs):
    pass


def passed(xs, after):
    return pl.pallas_call(
        pass_kernel,
        out_shape=[jax.ShapeDtypeStruct(x.shape, x.dtype) for x in xs],
        in_specs=[ANYWHERE] * (len(xs) + len(after)),
        out_specs=[ANYWHERE] * len(xs),
        input_output_aliases={i: i for i in range(len(xs))},
        compiler_params=pltpu.CompilerParams(vmem_limit_bytes=ROOM),
    )(*xs, *after)


def gate_kernel(*refs):
    refs[-1][...] = jnp.zeros_like(refs[-1])


def gate(after, flops):
    return pl.pallas_call(
        gate_kernel,
        out_shape=jax.ShapeDtypeStruct((8, 128), jnp.float32),
        in_specs=[ANYWHERE] * len(after),
        out_specs=IN_VMEM,
        compiler_params=pltpu.CompilerParams(vmem_limit_bytes=ROOM),
        cost_estimate=pl.CostEstimate(flops=flops, bytes_accessed=0, transcendentals=0),
    )(*after)


def deep_kernel(w, t0, t1, out_ref, total):
    step = pl.program_id(0)

    @pl.when(step == 0)
    def _():
        total[...] = jnp.zeros_like(total)

    rows = t0.shape[0]
    for k, t in enumerate((t0, t1)):
        total[:, k * rows : (k + 1) * rows] += lax.dot_general(
            w[...], t[...], BOTH_LAST, preferred_element_type=jnp.float32
        )

    @pl.when(step == pl.num_programs(0) - 1)
    def _():
        out_ref[...] = total[...].astype(out_ref.dtype)


def deep_product(w, t0, t1):
    m, depth = w.shape
    rows = t0.shape[0]
    block = divisor(depth, 3584)
    return pl.pallas_call(
        deep_kernel,
        grid=(depth // block,),
        in_specs=[pl.BlockSpec((m, block), lambda i: (0, i))] + [pl.BlockSpec((rows, block), lambda i: (0, i))] * 2,
        out_specs=pl.BlockSpec((m, 2 * rows), lambda i: (0, 0)),
        out_shape=jax.ShapeDtypeStruct((m, 2 * rows), jnp.bfloat16),
        scratch_shapes=[pltpu.VMEM((m, 2 * rows), jnp.float32)],
        compiler_params=pltpu.CompilerParams(vmem_limit_bytes=ROOM),
        cost_estimate=pl.CostEstimate(
            flops=4 * m * rows * depth, bytes_accessed=2 * depth * (m + 2 * rows), transcendentals=0
        ),
    )(*[pltpu.with_memory_space_constraint(x, pltpu.HBM) for x in (w, t0)], t1)


def product_kernel(plan, *refs):
    outs = refs[len(refs) - len(plan) :]
    for out, (ws, ts) in zip(outs, plan):
        for i, (w,) in enumerate(ws):
            for k, pieces in enumerate(ts):
                total, start = 0.0, 0
                for t in pieces:
                    rows, width = refs[t].shape
                    total += lax.dot_general(
                        refs[w][:, start : start + width],
                        refs[t][...],
                        BOTH_LAST,
                        preferred_element_type=jnp.float32,
                    )
                    start += width
                out[i, :, k * rows : (k + 1) * rows] = total.astype(out.dtype)


def products(jobs, dtype, after, flops=0):
    arrays, plan, shapes = [], [], []
    for ws, ts in jobs:
        places = []
        for group in ([(w,) for w in ws], ts):
            place = []
            for x in group:
                at = []
                for piece in x:
                    known = [i for i, y in enumerate(arrays) if y is piece]
                    if not known:
                        arrays.append(piece)
                    at.append(known[0] if known else len(arrays) - 1)
                place.append(tuple(at))
            places.append(place)
        plan.append(tuple(places))
        shapes.append((len(ws), ws[0].shape[0], sum(t[0].shape[0] for t in ts)))
    size = sum(a * b * c for a, b, c in shapes)
    return pl.pallas_call(
        functools.partial(product_kernel, plan),
        in_specs=[IN_VMEM] * len(arrays) + [ANYWHERE] * len(after),
        out_specs=[IN_VMEM] * len(jobs),
        out_shape=[jax.ShapeDtypeStruct(shape, dtype) for shape in shapes],
        compiler_params=pltpu.CompilerParams(vmem_limit_bytes=ROOM),
        cost_estimate=pl.CostEstimate(flops=flops + size, bytes_accessed=size, transcendentals=0),
    )(*arrays, *after)


def add_kernel(n, *refs):
    out = refs[-1]
    for i in range(n):
        out[i : i + 1] = (refs[i][...] + refs[n + i][...].astype(jnp.float32)).astype(out.dtype)


def added(mine, came, dtype):
    shape = (len(mine), *mine[0].shape[1:])
    size = shape[0] * shape[1] * shape[2]
    return pl.pallas_call(
        functools.partial(add_kernel, len(mine)),
        in_specs=[IN_VMEM] * (2 * len(mine)),
        out_specs=IN_VMEM,
        out_shape=jax.ShapeDtypeStruct(shape, dtype),
        compiler_params=pltpu.CompilerParams(vmem_limit_bytes=ROOM),
        cost_estimate=pl.CostEstimate(flops=size, bytes_accessed=size, transcendentals=0),
    )(*mine, *came)


def total_kernel(n_out, n_terms, *refs):
    outs = refs[-n_out:]
    rows = outs[0].shape[1]
    for k, out in enumerate(outs):
        part = slice(k * rows, (k + 1) * rows)
        total = refs[0][0, :, part]
        for term in refs[1:n_terms]:
            total = total + term[0, :, part].astype(jnp.float32)
        out[...] = total.astype(out.dtype)


def totals(terms, rows, after):
    _, m, width = terms[0].shape
    return pl.pallas_call(
        functools.partial(total_kernel, width // rows, len(terms)),
        in_specs=[IN_VMEM] * len(terms) + [ANYWHERE] * len(after),
        out_specs=[IN_VMEM] * (width // rows),
        out_shape=[jax.ShapeDtypeStruct((m, rows), jnp.bfloat16)] * (width // rows),
        compiler_params=pltpu.CompilerParams(vmem_limit_bytes=ROOM),
        cost_estimate=pl.CostEstimate(flops=m * width, bytes_accessed=m * width, transcendentals=0),
    )(*terms, *after)


def join_kernel(places, *refs):
    n = len(places)
    part_refs, bias_ref, out_ref, joined = refs[:n], refs[n], refs[n + 1], refs[n + 2]
    me = lax.axis_index("row")
    plane, core = me // 2, me % 2
    for (came, other), part in zip(places, part_refs):
        m = part.shape[0]
        source = functools.reduce(lambda x, p: jnp.where(plane == p, came[p], x), range(1, len(came)), came[0])
        start = pl.multiple_of((2 * source + (core ^ other)) * m, 8)
        joined[pl.ds(start, m), :] = part[...].astype(jnp.float32)
    block = divisor(out_ref.shape[1], 512)
    for i in range(out_ref.shape[1] // block):
        cols = slice(i * block, (i + 1) * block)
        out_ref[:, cols] = (joined[cols, :].T + bias_ref[:, cols]).astype(out_ref.dtype)


def join(parts, rows, bias):
    width = bias.shape[0]
    return pl.pallas_call(
        functools.partial(join_kernel, [(came, other) for came, other, _ in parts]),
        out_shape=jax.ShapeDtypeStruct((rows, width), jnp.bfloat16),
        in_specs=[IN_VMEM] * (len(parts) + 1),
        out_specs=IN_VMEM,
        scratch_shapes=[pltpu.VMEM((width, rows), jnp.float32)],
        compiler_params=pltpu.CompilerParams(vmem_limit_bytes=ROOM),
        cost_estimate=pl.CostEstimate(flops=width * rows, bytes_accessed=4 * width * rows, transcendentals=0),
    )(*[part for _, _, part in parts], bias[None, :])


def chain(own, planes, send, after):
    (own,) = own
    held = []
    last = {0: own, 1: own}
    second = []
    for s in range(1, planes):
        if s == 2:
            last = dict(enumerate(passed([last[0], last[1]], after)))
            held = [(last[i], came) for i, (_, came) in enumerate(held)]
        now = {}
        for parity in (0, 1):
            pairs, came = [], {}
            for p in range(parity, planes - 1, 2):
                if p - s + 1 >= 0:
                    pairs.append((p, p + 1))
                    came[p + 1] = p - s + 1
                if p + s < planes:
                    pairs.append((p + 1, p))
                    came[p] = p + s
            if pairs:
                now[parity] = send(last[1 - parity], pairs)
                held.append((now[parity], came))
                if s == 2:
                    second.append(now[parity])
        last = now
    slots = []
    for d in range(planes - 2, 0, -1) if planes > 2 else ():
        slots.append(d)
    found = []
    for d in slots + [planes - 1]:
        wanted = [next(i for i, (_, came) in enumerate(held) if came.get(p) == p ^ d) for p in range(planes)]
        used = sorted(set(wanted))
        found.append(([[held[i][0]] for i in used], [used.index(i) for i in wanted], [p ^ d for p in range(planes)]))
    return found, second


def line_of_four(own, send, after):
    ends = [0, 1, 1, 0]
    swap = [(0, 1), (1, 0), (2, 3), (3, 2)]
    cross = [send(piece, [(0, 3), (3, 0)]) for piece in own]
    (out,) = choose([cross, own], ends, after)
    near = send(out, swap)
    inner = send(out, [(1, 2), (2, 1)])
    (out,) = choose([own, [inner]], ends, [])
    final = send(out, swap)
    slots = [
        ([cross, [inner]], ends, [3, 2, 1, 0]),
        ([[near]], [0, 0, 0, 0], [1, 3, 0, 2]),
        ([[final]], [0, 0, 0, 0], [2, 0, 3, 1]),
    ]
    return slots, [near, inner]


def shards(tokens, qkv_weight, qkv_bias):
    n_row, n_col = lax.axis_size("row"), lax.axis_size("col")
    planes = n_row // 2
    half, feats = tokens.shape
    weight = qkv_weight.reshape(feats, -1).T
    columns = weight.shape[0]

    def flip_col(x, j):
        return lax.ppermute(x, "col", [(i, i ^ j) for i in range(n_col)])

    def flip_row(x, j):
        return lax.ppermute(x, "row", [(i, i ^ j) for i in range(n_row)])

    js = list(range(n_col))
    cuts = CUTS if n_row == 8 else 1
    *own, far = bands(
        [tokens, weight], [(0, 0, part, cuts) for part in range(cuts)] + [(1, n_col - 1, 0, 1)], n_col, []
    )
    near = bands([weight], [(0, j, 0, 1) for j in js[:-1]], n_col, [far])
    w_band = [near[0]] + [flip_col(x, j) for j, x in zip(js[1:], list(near[1:]) + [far])]
    here = deep_product(weight, tokens, flip_row(tokens, 1))
    here_other = flip_row(here[:, half:], 1)
    everyone = list(range(planes))
    parts = [(everyone, 0, here[:, :half]), (everyone, 1, here_other)]

    def send(x, pairs):
        return lax.ppermute(x, "row", [(2 * a + c, 2 * b + c) for a, b in pairs for c in (0, 1)])

    if planes == 4:
        slots, second = line_of_four(own, send, [here_other, near[0]])
    else:
        slots, second = chain(own, planes, send, [here_other, near[0]])

    def arrived(slot, after, cuts=1):
        arrays, wanted, _ = slot
        value = choose(arrays, wanted, after, cuts)
        return [tuple(value), tuple(flip_row(x, 1) for x in value)]

    def apart(x):
        return [x] if x.shape[0] == 1 else [x[i : i + 1] for i in range(x.shape[0])]

    def halve(kept, mine, came, orders):
        for n, bit in enumerate(orders):
            go = [i for i, j in enumerate(kept) if j & bit]
            stay = [i for i, j in enumerate(kept) if not j & bit]
            got = flip_col(added([mine[i] for i in go], [came[i] for i in go], jnp.bfloat16), bit)
            kept = [kept[i] for i in stay]
            if n + 1 == len(orders):
                return [mine[stay[0]], came[stay[0]], got]
            mine = [added([mine[i]], [came[i]], jnp.float32) for i in stay]
            came = apart(got)
        return [mine[0], came[0]]

    bits = [1 << b for b in range(n_col.bit_length() - 1)]
    orders = [bits[i % len(bits) :] + bits[: i % len(bits)] for i in range(planes + 1)]
    splits = [([j for j in js if j & o[0]], [j for j in js if not j & o[0]]) for o in orders]
    last_j = n_col - 1

    early = list(range(planes - 2))
    late_in = flip_row(choose([[second[-1]]], [0] * planes, [], 14)[0], 1)
    blocks = {d: arrived(slots[d], second + [w_band[last_j]] + [late_in] * (not d), XCUTS if d else 1) for d in early}
    firsts = products([([w_band[last_j]], blocks[d]) for d in early], jnp.bfloat16, [])
    got_first = [flip_col(x, orders[i][0]) for i, x in enumerate(firsts)]
    nexts = products(
        [([w_band[j] for j in splits[i][0] if j != last_j], blocks[d]) for i, d in enumerate(early)],
        jnp.bfloat16,
        list(firsts[:1]),
    )
    got_next = [flip_col(x, orders[i][0]) for i, x in enumerate(nexts)]
    passing = [[j for j in splits[i][1] if len(orders[i]) > 1 and j & orders[i][1]] for i in early]
    staying = [[j for j in splits[i][1] if j not in passing[i]] for i in early]
    mine_of, first_mine = {}, list(nexts[:1])
    for which, flops in ((passing, KEPT), (staying, 0)):
        mines = products(
            [([w_band[j]], blocks[d]) for i, d in enumerate(early) for j in which[i]], jnp.float32, first_mine, flops
        )
        first_mine = list(mines[:1])
        mine_of.update(zip([(i, j) for i in early for j in which[i]], mines))

    def gather_sums(i, far, near):
        came = {last_j: far}
        came.update(zip([j for j in splits[i][0] if j != last_j], apart(near)))
        return [came[j | orders[i][0]] for j in splits[i][1]]

    n_kept = n_col // 2
    ended = []
    for i, d in enumerate(early):
        sums = gather_sums(i, got_first[i], got_next[i])
        ended.append(totals(halve(splits[i][1], [mine_of[i, j] for j in splits[i][1]], sums, orders[i][1:]), half, []))
    swapped = [flip_row(other, 1) for _, other in ended[1:]]
    both = arrived(slots[-1], [x for pair in ended for x in pair])
    backs = []
    for i, slot in enumerate(slots[:-1]):
        home = [(p, c) for p, c in enumerate(slot[2])]
        source = [slot[2].index(c) for c in everyone]
        if i:
            back = send(jnp.stack([ended[i][0], swapped[i - 1]]), home)
            backs.append(back)
            parts.append((source, 1, back[1]))
        else:
            back = send(jnp.stack(ended[i]), home)
            hop = flip_row(jnp.concatenate([back[1], back[1][:, : half // 2]], axis=1), 1)
            parts.append((source, 1, hop[:, :half]))
        parts.append((source, 0, back[0]))
    sents = first_mine
    late = []
    for core in (0, 1):
        i = len(early) + core
        near_js = [j for j in splits[i][0] if j != last_j]
        sents = products(
            [([w_band[last_j]], [both[core]]), ([w_band[j] for j in near_js], [both[core]])], jnp.bfloat16, sents[:1]
        )
        late.append((i, core, [flip_col(x, orders[i][0]) for x in sents]))
    late_mines = products(
        [([w_band[j]], [both[core]]) for i, core, _ in late for j in splits[i][1]], jnp.float32, list(sents[:1])
    )
    for i, core, got in late:
        mine = late_mines[core * n_kept : (core + 1) * n_kept]
        (done,) = totals(halve(splits[i][1], mine, gather_sums(i, *got), orders[i][1:]), half, [])
        home = [(2 * p + c, 2 * q + (c ^ core)) for p, q in enumerate(slots[-1][2]) for c in (0, 1)]
        source = [slots[-1][2].index(q) for q in everyone]
        parts.append((source, core, lax.ppermute(done, "row", home)))
    return join(parts, half, qkv_bias)


def solution(mesh):
    return jax.shard_map(
        shards,
        mesh=mesh,
        in_specs=(P("row", None), P(None, "col", "row", None), P("col")),
        out_specs=P("row", "col"),
        check_vma=False,
    )
```

```python
import functools

import jax
import jax.numpy as jnp
from jax import lax
from jax.experimental import pallas as pl
from jax.experimental.pallas import tpu as pltpu
from jax.sharding import PartitionSpec as P

ROOM = 14 * 1024 * 1024
KEPT = 0
BACKS = 0
CUTS = 1
XCUTS = 1
IN_VMEM = pl.BlockSpec(memory_space=pltpu.VMEM)
IN_HBM = pl.BlockSpec(memory_space=pltpu.HBM)
ANYWHERE = pl.BlockSpec(memory_space=pl.ANY)
BOTH_LAST = (((1,), (1,)), ((), ()))


def divisor(size, most):
    return max(d for d in range(128, most + 1, 128) if size % d == 0)


def bands_kernel(pieces, n_col, *refs):
    outs, sems = refs[-1 - len(pieces) : -1], refs[-1]
    col = lax.axis_index("col")
    copies = []
    for i, (which, j, part) in enumerate(pieces):
        band, width = refs[which].shape[1] // n_col, outs[i].shape[1]
        start = pl.multiple_of((col ^ j) * band + part * width, 128)
        copies.append(pltpu.make_async_copy(refs[which].at[:, pl.ds(start, width)], outs[i], sems.at[i]))
    for copy in copies:
        copy.start()
    for copy in copies:
        copy.wait()


def bands(xs, pieces, n_col, after):
    shapes = [(xs[which].shape[0], xs[which].shape[1] // n_col // parts) for which, _, _, parts in pieces]
    return pl.pallas_call(
        functools.partial(bands_kernel, [piece[:3] for piece in pieces], n_col),
        out_shape=[jax.ShapeDtypeStruct(shape, xs[piece[0]].dtype) for shape, piece in zip(shapes, pieces)],
        in_specs=[IN_HBM] * len(xs) + [ANYWHERE] * len(after),
        out_specs=[IN_VMEM] * len(pieces),
        scratch_shapes=[pltpu.SemaphoreType.DMA((len(pieces),))],
        compiler_params=pltpu.CompilerParams(vmem_limit_bytes=ROOM),
    )(*[pltpu.with_memory_space_constraint(x, pltpu.HBM) for x in xs], *after)


def choose_kernel(wanted, counts, cuts, *refs):
    outs, sem = refs[-1 - cuts : -1], refs[-1]
    plane = lax.axis_index("row") // 2
    at = 0
    for i, count in enumerate(counts):
        pieces = refs[at : at + count]
        at += count
        here = functools.reduce(jnp.logical_or, [plane == p for p, w in enumerate(wanted) if w == i])

        @pl.when(here)
        def _():
            n = max(count, cuts)
            width = pieces[0].shape[1] * count // n
            copies = []
            for k in range(n):
                source, from_col = k * count // n, k * width % pieces[0].shape[1]
                target, to_col = k * cuts // n, k * width % outs[0].shape[1]
                copies.append(
                    pltpu.make_async_copy(
                        pieces[source].at[:, pl.ds(from_col, width)], outs[target].at[:, pl.ds(to_col, width)], sem.at[k]
                    )
                )
            for copy in copies:
                copy.start()
            for copy in copies:
                copy.wait()


def choose(xs, wanted, after, cuts=1):
    flat = [piece for x in xs for piece in x]
    counts = [len(x) for x in xs]
    shape = (flat[0].shape[0], sum(piece.shape[1] for piece in xs[0]) // cuts)
    return pl.pallas_call(
        lambda *refs: choose_kernel(wanted, counts, cuts, *refs[: len(flat)], *refs[len(flat) + len(after) :]),
        out_shape=[jax.ShapeDtypeStruct(shape, flat[0].dtype)] * cuts,
        in_specs=[ANYWHERE] * (len(flat) + len(after)),
        out_specs=[IN_VMEM] * cuts,
        scratch_shapes=[pltpu.SemaphoreType.DMA((max(counts + [cuts]),))],
        compiler_params=pltpu.CompilerParams(vmem_limit_bytes=ROOM),
    )(*flat, *after)


def pass_kernel(*refs):
    pass


def passed(xs, after):
    return pl.pallas_call(
        pass_kernel,
        out_shape=[jax.ShapeDtypeStruct(x.shape, x.dtype) for x in xs],
        in_specs=[ANYWHERE] * (len(xs) + len(after)),
        out_specs=[ANYWHERE] * len(xs),
        input_output_aliases={i: i for i in range(len(xs))},
        compiler_params=pltpu.CompilerParams(vmem_limit_bytes=ROOM),
    )(*xs, *after)


def gate_kernel(*refs):
    refs[-1][...] = jnp.zeros_like(refs[-1])


def gate(after, flops):
    return pl.pallas_call(
        gate_kernel,
        out_shape=jax.ShapeDtypeStruct((8, 128), jnp.float32),
        in_specs=[ANYWHERE] * len(after),
        out_specs=IN_VMEM,
        compiler_params=pltpu.CompilerParams(vmem_limit_bytes=ROOM),
        cost_estimate=pl.CostEstimate(flops=flops, bytes_accessed=0, transcendentals=0),
    )(*after)


def deep_kernel(w, t0, t1, out_ref, total):
    step = pl.program_id(0)

    @pl.when(step == 0)
    def _():
        total[...] = jnp.zeros_like(total)

    rows = t0.shape[0]
    for k, t in enumerate((t0, t1)):
        total[:, k * rows : (k + 1) * rows] += lax.dot_general(
            w[...], t[...], BOTH_LAST, preferred_element_type=jnp.float32
        )

    @pl.when(step == pl.num_programs(0) - 1)
    def _():
        out_ref[...] = total[...].astype(out_ref.dtype)


def deep_product(w, t0, t1):
    m, depth = w.shape
    rows = t0.shape[0]
    block = divisor(depth, 3584)
    return pl.pallas_call(
        deep_kernel,
        grid=(depth // block,),
        in_specs=[pl.BlockSpec((m, block), lambda i: (0, i))] + [pl.BlockSpec((rows, block), lambda i: (0, i))] * 2,
        out_specs=pl.BlockSpec((m, 2 * rows), lambda i: (0, 0)),
        out_shape=jax.ShapeDtypeStruct((m, 2 * rows), jnp.bfloat16),
        scratch_shapes=[pltpu.VMEM((m, 2 * rows), jnp.float32)],
        compiler_params=pltpu.CompilerParams(vmem_limit_bytes=ROOM),
        cost_estimate=pl.CostEstimate(
            flops=4 * m * rows * depth, bytes_accessed=2 * depth * (m + 2 * rows), transcendentals=0
        ),
    )(*[pltpu.with_memory_space_constraint(x, pltpu.HBM) for x in (w, t0)], t1)


def product_kernel(plan, *refs):
    outs = refs[len(refs) - len(plan) :]
    for out, (ws, ts) in zip(outs, plan):
        for i, (w,) in enumerate(ws):
            for k, pieces in enumerate(ts):
                total, start = 0.0, 0
                for t in pieces:
                    rows, width = refs[t].shape
                    total += lax.dot_general(
                        refs[w][:, start : start + width],
                        refs[t][...],
                        BOTH_LAST,
                        preferred_element_type=jnp.float32,
                    )
                    start += width
                out[i, :, k * rows : (k + 1) * rows] = total.astype(out.dtype)


def products(jobs, dtype, after, flops=0):
    arrays, plan, shapes = [], [], []
    for ws, ts in jobs:
        places = []
        for group in ([(w,) for w in ws], ts):
            place = []
            for x in group:
                at = []
                for piece in x:
                    known = [i for i, y in enumerate(arrays) if y is piece]
                    if not known:
                        arrays.append(piece)
                    at.append(known[0] if known else len(arrays) - 1)
                place.append(tuple(at))
            places.append(place)
        plan.append(tuple(places))
        shapes.append((len(ws), ws[0].shape[0], sum(t[0].shape[0] for t in ts)))
    size = sum(a * b * c for a, b, c in shapes)
    return pl.pallas_call(
        functools.partial(product_kernel, plan),
        in_specs=[IN_VMEM] * len(arrays) + [ANYWHERE] * len(after),
        out_specs=[IN_VMEM] * len(jobs),
        out_shape=[jax.ShapeDtypeStruct(shape, dtype) for shape in shapes],
        compiler_params=pltpu.CompilerParams(vmem_limit_bytes=ROOM),
        cost_estimate=pl.CostEstimate(flops=flops + size, bytes_accessed=size, transcendentals=0),
    )(*arrays, *after)


def add_kernel(n, *refs):
    out = refs[-1]
    for i in range(n):
        out[i : i + 1] = (refs[i][...] + refs[n + i][...].astype(jnp.float32)).astype(out.dtype)


def added(mine, came, dtype):
    shape = (len(mine), *mine[0].shape[1:])
    size = shape[0] * shape[1] * shape[2]
    return pl.pallas_call(
        functools.partial(add_kernel, len(mine)),
        in_specs=[IN_VMEM] * (2 * len(mine)),
        out_specs=IN_VMEM,
        out_shape=jax.ShapeDtypeStruct(shape, dtype),
        compiler_params=pltpu.CompilerParams(vmem_limit_bytes=ROOM),
        cost_estimate=pl.CostEstimate(flops=size, bytes_accessed=size, transcendentals=0),
    )(*mine, *came)


def total_kernel(n_out, n_terms, *refs):
    outs = refs[-n_out:]
    rows = outs[0].shape[1]
    for k, out in enumerate(outs):
        part = slice(k * rows, (k + 1) * rows)
        total = refs[0][0, :, part]
        for term in refs[1:n_terms]:
            total = total + term[0, :, part].astype(jnp.float32)
        out[...] = total.astype(out.dtype)


def totals(terms, rows, after):
    _, m, width = terms[0].shape
    return pl.pallas_call(
        functools.partial(total_kernel, width // rows, len(terms)),
        in_specs=[IN_VMEM] * len(terms) + [ANYWHERE] * len(after),
        out_specs=[IN_VMEM] * (width // rows),
        out_shape=[jax.ShapeDtypeStruct((m, rows), jnp.bfloat16)] * (width // rows),
        compiler_params=pltpu.CompilerParams(vmem_limit_bytes=ROOM),
        cost_estimate=pl.CostEstimate(flops=m * width, bytes_accessed=m * width, transcendentals=0),
    )(*terms, *after)


def join_kernel(places, *refs):
    n = len(places)
    part_refs, bias_ref, out_ref, joined = refs[:n], refs[n], refs[n + 1], refs[n + 2]
    me = lax.axis_index("row")
    plane, core = me // 2, me % 2
    for (came, other), part in zip(places, part_refs):
        m = part.shape[0]
        source = functools.reduce(lambda x, p: jnp.where(plane == p, came[p], x), range(1, len(came)), came[0])
        start = pl.multiple_of((2 * source + (core ^ other)) * m, 8)
        joined[pl.ds(start, m), :] = part[...].astype(jnp.float32)
    block = divisor(out_ref.shape[1], 512)
    for i in range(out_ref.shape[1] // block):
        cols = slice(i * block, (i + 1) * block)
        out_ref[:, cols] = (joined[cols, :].T + bias_ref[:, cols]).astype(out_ref.dtype)


def join(parts, rows, bias):
    width = bias.shape[0]
    return pl.pallas_call(
        functools.partial(join_kernel, [(came, other) for came, other, _ in parts]),
        out_shape=jax.ShapeDtypeStruct((rows, width), jnp.bfloat16),
        in_specs=[IN_VMEM] * (len(parts) + 1),
        out_specs=IN_VMEM,
        scratch_shapes=[pltpu.VMEM((width, rows), jnp.float32)],
        compiler_params=pltpu.CompilerParams(vmem_limit_bytes=ROOM),
        cost_estimate=pl.CostEstimate(flops=width * rows, bytes_accessed=4 * width * rows, transcendentals=0),
    )(*[part for _, _, part in parts], bias[None, :])


def chain(own, planes, send, after):
    (own,) = own
    held = []
    last = {0: own, 1: own}
    second = []
    for s in range(1, planes):
        if s == 2:
            last = dict(enumerate(passed([last[0], last[1]], after)))
            held = [(last[i], came) for i, (_, came) in enumerate(held)]
        now = {}
        for parity in (0, 1):
            pairs, came = [], {}
            for p in range(parity, planes - 1, 2):
                if p - s + 1 >= 0:
                    pairs.append((p, p + 1))
                    came[p + 1] = p - s + 1
                if p + s < planes:
                    pairs.append((p + 1, p))
                    came[p] = p + s
            if pairs:
                now[parity] = send(last[1 - parity], pairs)
                held.append((now[parity], came))
                if s == 2:
                    second.append(now[parity])
        last = now
    slots = []
    for d in range(planes - 2, 0, -1) if planes > 2 else ():
        slots.append(d)
    found = []
    for d in slots + [planes - 1]:
        wanted = [next(i for i, (_, came) in enumerate(held) if came.get(p) == p ^ d) for p in range(planes)]
        used = sorted(set(wanted))
        found.append(([[held[i][0]] for i in used], [used.index(i) for i in wanted], [p ^ d for p in range(planes)]))
    return found, second


def line_of_four(own, send, after):
    ends = [0, 1, 1, 0]
    swap = [(0, 1), (1, 0), (2, 3), (3, 2)]
    cross = [send(piece, [(0, 3), (3, 0)]) for piece in own]
    (out,) = choose([cross, own], ends, after)
    near = send(out, swap)
    inner = send(out, [(1, 2), (2, 1)])
    (out,) = choose([own, [inner]], ends, [])
    final = send(out, swap)
    slots = [
        ([cross, [inner]], ends, [3, 2, 1, 0]),
        ([[near]], [0, 0, 0, 0], [1, 3, 0, 2]),
        ([[final]], [0, 0, 0, 0], [2, 0, 3, 1]),
    ]
    return slots, [near, inner]


def shards(tokens, qkv_weight, qkv_bias):
    n_row, n_col = lax.axis_size("row"), lax.axis_size("col")
    planes = n_row // 2
    half, feats = tokens.shape
    weight = qkv_weight.reshape(feats, -1).T
    columns = weight.shape[0]

    def flip_col(x, j):
        return lax.ppermute(x, "col", [(i, i ^ j) for i in range(n_col)])

    def flip_row(x, j):
        return lax.ppermute(x, "row", [(i, i ^ j) for i in range(n_row)])

    js = list(range(n_col))
    cuts = CUTS if n_row == 8 else 1
    *own, far = bands(
        [tokens, weight], [(0, 0, part, cuts) for part in range(cuts)] + [(1, n_col - 1, 0, 1)], n_col, []
    )
    near = bands([weight], [(0, j, 0, 1) for j in js[:-1]], n_col, [far])
    w_band = [near[0]] + [flip_col(x, j) for j, x in zip(js[1:], list(near[1:]) + [far])]
    here = deep_product(weight, tokens, flip_row(tokens, 1))
    here_other = flip_row(here[:, half:], 1)
    everyone = list(range(planes))
    parts = [(everyone, 0, here[:, :half]), (everyone, 1, here_other)]

    def send(x, pairs):
        return lax.ppermute(x, "row", [(2 * a + c, 2 * b + c) for a, b in pairs for c in (0, 1)])

    if planes == 4:
        slots, second = line_of_four(own, send, [here_other, near[0]])
    else:
        slots, second = chain(own, planes, send, [here_other, near[0]])

    def arrived(slot, after, cuts=1):
        arrays, wanted, _ = slot
        value = choose(arrays, wanted, after, cuts)
        return [tuple(value), tuple(flip_row(x, 1) for x in value)]

    def apart(x):
        return [x] if x.shape[0] == 1 else [x[i : i + 1] for i in range(x.shape[0])]

    def halve(kept, mine, came, orders):
        for n, bit in enumerate(orders):
            go = [i for i, j in enumerate(kept) if j & bit]
            stay = [i for i, j in enumerate(kept) if not j & bit]
            got = flip_col(added([mine[i] for i in go], [came[i] for i in go], jnp.bfloat16), bit)
            kept = [kept[i] for i in stay]
            if n + 1 == len(orders):
                return [mine[stay[0]], came[stay[0]], got]
            mine = [added([mine[i]], [came[i]], jnp.float32) for i in stay]
            came = apart(got)
        return [mine[0], came[0]]

    bits = [1 << b for b in range(n_col.bit_length() - 1)]
    orders = [bits[i % len(bits) :] + bits[: i % len(bits)] for i in range(planes + 1)]
    splits = [([j for j in js if j & o[0]], [j for j in js if not j & o[0]]) for o in orders]
    last_j = n_col - 1

    early = list(range(planes - 2))
    late_in = flip_row(choose([[second[-1]]], [0] * planes, [], 14)[0], 1)
    blocks = {d: arrived(slots[d], second + [w_band[last_j]] + [late_in] * (not d), XCUTS if d else 1) for d in early}
    firsts = products([([w_band[last_j]], blocks[d]) for d in early], jnp.bfloat16, [])
    got_first = [flip_col(x, orders[i][0]) for i, x in enumerate(firsts)]
    nexts = products(
        [([w_band[j] for j in splits[i][0] if j != last_j], blocks[d]) for i, d in enumerate(early)],
        jnp.bfloat16,
        list(firsts[:1]),
    )
    got_next = [flip_col(x, orders[i][0]) for i, x in enumerate(nexts)]
    passing = [[j for j in splits[i][1] if len(orders[i]) > 1 and j & orders[i][1]] for i in early]
    staying = [[j for j in splits[i][1] if j not in passing[i]] for i in early]
    mine_of, first_mine = {}, list(nexts[:1])
    for which, flops in ((passing, KEPT), (staying, 0)):
        mines = products(
            [([w_band[j]], blocks[d]) for i, d in enumerate(early) for j in which[i]], jnp.float32, first_mine, flops
        )
        first_mine = list(mines[:1])
        mine_of.update(zip([(i, j) for i in early for j in which[i]], mines))

    def gather_sums(i, far, near):
        came = {last_j: far}
        came.update(zip([j for j in splits[i][0] if j != last_j], apart(near)))
        return [came[j | orders[i][0]] for j in splits[i][1]]

    n_kept = n_col // 2
    ended = []
    for i, d in enumerate(early):
        sums = gather_sums(i, got_first[i], got_next[i])
        ended.append(totals(halve(splits[i][1], [mine_of[i, j] for j in splits[i][1]], sums, orders[i][1:]), half, []))
    swapped = [flip_row(other, 1) for _, other in ended[1:]]
    both = arrived(slots[-1], [x for pair in ended for x in pair])
    backs = []
    for i, slot in enumerate(slots[:-1]):
        home = [(p, c) for p, c in enumerate(slot[2])]
        source = [slot[2].index(c) for c in everyone]
        if i:
            back = send(jnp.stack([ended[i][0], swapped[i - 1]]), home)
            backs.append(back)
            parts.append((source, 1, back[1]))
        else:
            back = send(jnp.stack(ended[i]), home)
            hop = flip_row(jnp.concatenate([back[1], back[1][:, : half // 2]], axis=1), 1)
            parts.append((source, 1, hop[:, :half]))
        parts.append((source, 0, back[0]))
    sents = first_mine
    late = []
    for core in (0, 1):
        i = len(early) + core
        near_js = [j for j in splits[i][0] if j != last_j]
        sents = products(
            [([w_band[last_j]], [both[core]]), ([w_band[j] for j in near_js], [both[core]])], jnp.bfloat16, sents[:1]
        )
        late.append((i, core, [flip_col(x, orders[i][0]) for x in sents]))
    late_mines = products(
        [([w_band[j]], [both[core]]) for i, core, _ in late for j in splits[i][1]], jnp.float32, list(sents[:1])
    )
    for i, core, got in late:
        mine = late_mines[core * n_kept : (core + 1) * n_kept]
        (done,) = totals(halve(splits[i][1], mine, gather_sums(i, *got), orders[i][1:]), half, [])
        home = [(2 * p + c, 2 * q + (c ^ core)) for p, q in enumerate(slots[-1][2]) for c in (0, 1)]
        source = [slots[-1][2].index(q) for q in everyone]
        parts.append((source, core, lax.ppermute(done, "row", home)))
    return join(parts, half, qkv_bias)


def solution(mesh):
    return jax.shard_map(
        shards,
        mesh=mesh,
        in_specs=(P("row", None), P(None, "col", "row", None), P("col")),
        out_specs=P("row", "col"),
        check_vma=False,
    )
```
